512 devices in a mesh: replica: 64 (over z, x), tensor: 8 (over y, core).
Axes of the slice: x: 4, y: 4, z: 16, core: 2. Of those that a mesh axis runs over, the one named last changes fastest.
Arguments:
- queries: bfloat16 [2048, 2, 8192], P('replica', None, 'tensor'), may hold values from -8.5 to 8.5, as said below
- fresh_entries: bfloat16 [2048, 2, 2, 1024], P('replica', None, None, 'tensor'), may hold values from -8.5 to 8.5, as said below
- suffix_page_pool: bfloat16 [16384, 16, 2, 1024], P('replica', None, None, 'tensor'), may hold values from -6 to 6
- page_table: int32 [2048, 8], P('replica'), may hold values from 0 to 16383, as said below
- suffix_len: int32 [2048], P('replica'), may hold values from 2 to 126, as said below
- prompt_key_value: bfloat16 [128, 64, 2, 1024], P('replica', None, None, 'tensor'), may hold values from -6 to 6
- prompt_len: int32 [128], P('replica'), may hold values from 2 to 64, as said below
- sibling_group: int32 [2048], P('replica'), may hold values from 0 to 127, as said below
- new_position: int32 [2048], P('replica'), may hold values from 0 to 2047, as said below
- output_weight: bfloat16 [8192, 8192], P('tensor', 'replica'), may hold values from -0.25 to 0.25
Outputs:
- moved_cache: bfloat16 [2048, 128, 2, 1024], P('replica', None, None, 'tensor')
- block_output: bfloat16 [2, 2048, 8192], P(None, 'tensor', 'replica')
The draws below stay inside these ranges and needn't reach their ends.
Inputs may be any that keep to these rules, and one draw needn't show every extreme that they name: page_table maps the pages of the siblings of replica r one to one onto pool pages r * 32 * 8 to (r + 1) * 32 * 8 - 1. `suffix_len`: lengths differ between replicas; the largest is reached. `prompt_len`: the largest is reached. `sibling_group`: A sibling at old position s lies on replica s // 32 and belongs to one of the groups r * 2 to (r + 1) * 2 - 1 of that replica r, whose prompts that replica holds; every group has at least one sibling. `new_position`: A permutation; the new position is a replica times 32 plus a slot. The 32 siblings of one replica go to 32 different replicas, and every replica receives exactly 32. `queries`: real values of order one. `fresh_entries`: real values of order one.
All inputs are finite; a program needn't handle non-finite values.
Results may differ from the reference program's by a relative error of at most 0.02.
Values may be sent and summed in bfloat16 or wider, within the bound.
A program may use at most 64 MiB of HBM per device.

```python
import math
import jax
import jax.numpy as jnp
from jax import lax

D = 8192
QUERY_HEADS = 64
KEY_VALUE_HEADS = 8
HEAD_SIZE = 128
PAGE_TOKENS = 16
SUF_PAGES = 8
PROMPT_TOKENS = 64
GROUPS_DEV = 2
DECODE_STEPS = 2
S_DEV = 32
SUFFIX_TOKENS = 128
SIBLING_TOTAL = 2048
GROUP_TOTAL = 128
SUFFIX_PAGES = 16384


def draw_queries(key, part):
    key = jax.random.fold_in(key, 5)
    decode_result = jnp.clip(jax.random.normal(key, (SIBLING_TOTAL, DECODE_STEPS, QUERY_HEADS * HEAD_SIZE), jnp.float32), -6.0, 6.0)
    return decode_result.astype(jnp.bfloat16)


def draw_fresh_entries(key, part):
    key = jax.random.fold_in(key, 6)
    decode_result = jnp.clip(jax.random.normal(key, (SIBLING_TOTAL, DECODE_STEPS, 2, KEY_VALUE_HEADS * HEAD_SIZE), jnp.float32), -6.0, 6.0)
    return decode_result.astype(jnp.bfloat16)


def draw_page_table(key, part):
    key = jax.random.fold_in(key, 7)
    replica_count = SIBLING_TOTAL // S_DEV
    local_pages = S_DEV * SUF_PAGES
    scores = jax.random.randint(key, (replica_count, local_pages), 0, 1 << 20) * local_pages + jnp.arange(local_pages)[None, :]
    ordering = jnp.argsort(scores, axis=1, stable=True)
    pages = ordering + jnp.arange(replica_count)[:, None] * local_pages
    return pages.reshape(SIBLING_TOTAL, SUF_PAGES).astype(jnp.int32)


def draw_suffix_len(key, part):
    key = jax.random.fold_in(key, 9)
    factor_key, length_key = jax.random.split(key)
    replica_count = SIBLING_TOTAL // S_DEV
    factor = jax.random.randint(factor_key, (replica_count, 1), 1, 9)
    raw_length = jax.random.randint(length_key, (replica_count, S_DEV), 0, SUFFIX_TOKENS - 3)
    lengths = 2 + raw_length * factor // 8
    lengths = lengths.reshape(SIBLING_TOTAL).at[0].set(SUFFIX_TOKENS - 2)
    return lengths.astype(jnp.int32)


def draw_prompt_len(key, part):
    key = jax.random.fold_in(key, 11)
    lengths = jax.random.randint(key, (GROUP_TOTAL,), 2, PROMPT_TOKENS + 1)
    return lengths.at[0].set(PROMPT_TOKENS).astype(jnp.int32)


def draw_sibling_group(key, part):
    key = jax.random.fold_in(key, 13)
    extra_key, shuffle_key = jax.random.split(key)
    replica_count = SIBLING_TOTAL // S_DEV
    slots = jnp.arange(S_DEV)[None, :]
    extra_group = jax.random.randint(extra_key, (replica_count, S_DEV), 0, GROUPS_DEV)
    local_group = jnp.where(slots < GROUPS_DEV, slots, extra_group)
    scores = jax.random.randint(shuffle_key, (replica_count, S_DEV), 0, 1 << 20) * S_DEV + slots
    ordering = jnp.argsort(scores, axis=1, stable=True)
    shuffled = jnp.take_along_axis(local_group, ordering, axis=1)
    groups = shuffled + jnp.arange(replica_count)[:, None] * GROUPS_DEV
    return groups.reshape(SIBLING_TOTAL).astype(jnp.int32)


def draw_new_position(key, part):
    key = jax.random.fold_in(key, 17)
    relabel_key, spread_key, offset_key, slot_key = jax.random.split(key, 4)
    replica_count = SIBLING_TOTAL // S_DEV
    relabel = jax.random.permutation(relabel_key, replica_count)
    spread = jax.random.permutation(spread_key, replica_count)
    offsets = jax.random.permutation(offset_key, replica_count)[:S_DEV]
    anchor = jnp.arange(replica_count)[:, None]
    destination = relabel[(spread[anchor] + offsets[None, :]) % replica_count]
    scores = jax.random.randint(slot_key, (replica_count, S_DEV), 0, 1 << 20) * S_DEV + jnp.arange(S_DEV)[None, :]
    ranking = jnp.argsort(jnp.argsort(scores, axis=1, stable=True), axis=1, stable=True)
    new_slot = ranking[destination, jnp.arange(S_DEV)[None, :]]
    positions = destination * S_DEV + new_slot
    return positions.reshape(SIBLING_TOTAL).astype(jnp.int32)


def shard_levels(stream_key, shape, shards, smallest, largest):
    def one(dim, blocks):
        steps = jax.random.uniform(jax.random.fold_in(jax.random.fold_in(stream_key, 6), dim), (blocks,), jnp.float32, smallest / len(shards), largest / len(shards))
        return jnp.repeat(jnp.exp(steps), shape[dim] // blocks).reshape((-1,) + (1,) * (len(shape) - dim - 1))

    gain = one(*shards[0])
    for cut in shards[1:]:
        gain = gain * one(*cut)
    return gain


def scatter_about(own_key, dims, width, bound, cuts=(), held_as=jnp.bfloat16):
    values = width * jax.random.normal(own_key, dims, jnp.float32)
    if cuts:
        values = values * shard_levels(own_key, dims, cuts, -0.22, 0.18)
    return jnp.clip(values, -bound, bound).astype(held_as)


def setup_inputs(seed: int = 0) -> dict:
    streams_of = jax.random.split(jax.random.key(seed), 11)
    queries = draw_queries(jax.random.fold_in(streams_of[10], 71), 0)
    fresh_entries = draw_fresh_entries(jax.random.fold_in(streams_of[10], 71), 0)
    suffix_page_pool = scatter_about(streams_of[2], (SUFFIX_PAGES, PAGE_TOKENS, 2, KEY_VALUE_HEADS * HEAD_SIZE), 1.0, 6.0, ((0, 64), (3, 8)))
    page_table = draw_page_table(jax.random.fold_in(streams_of[10], 71), 0)
    suffix_len = draw_suffix_len(jax.random.fold_in(streams_of[10], 71), 0)
    prompt_key_value = scatter_about(streams_of[5], (GROUP_TOTAL, PROMPT_TOKENS, 2, KEY_VALUE_HEADS * HEAD_SIZE), 1.0, 6.0, ((0, 64), (3, 8)))
    prompt_len = draw_prompt_len(jax.random.fold_in(streams_of[10], 71), 0)
    sibling_group = draw_sibling_group(jax.random.fold_in(streams_of[10], 71), 0)
    new_position = draw_new_position(jax.random.fold_in(streams_of[10], 71), 0)
    output_weight = scatter_about(streams_of[9], (QUERY_HEADS * HEAD_SIZE, D), (QUERY_HEADS * HEAD_SIZE // 16) ** -0.5, 0.25, ((0, 8), (1, 64)))
    return {"queries": queries, "fresh_entries": fresh_entries, "suffix_page_pool": suffix_page_pool, "page_table": page_table, "suffix_len": suffix_len, "prompt_key_value": prompt_key_value, "prompt_len": prompt_len, "sibling_group": sibling_group, "new_position": new_position, "output_weight": output_weight}


masked_score = -1e+30

def reference(queries, fresh_entries, suffix_page_pool, page_table, suffix_len, prompt_key_value, prompt_len, sibling_group, new_position, output_weight):
    key_value_width = KEY_VALUE_HEADS * HEAD_SIZE
    group_members = QUERY_HEADS // KEY_VALUE_HEADS
    pages = suffix_page_pool[page_table]
    suffix_cache = pages.reshape(SIBLING_TOTAL, SUFFIX_TOKENS, 2, key_value_width)
    position = jnp.arange(SUFFIX_TOKENS, dtype=jnp.int32)[None, :]
    length = suffix_len[:, None]
    suffix_cache = jnp.where((position < length)[:, :, None, None], suffix_cache, jnp.zeros((), suffix_cache.dtype))
    for step_index in range(DECODE_STEPS):
        fresh_spot = (position == length + step_index)[:, :, None, None]
        suffix_cache = jnp.where(fresh_spot, fresh_entries[:, step_index][:, None], suffix_cache)

    def attend_one(sibling_items):
        query_row_block, cache_rows, group_index, own_length = sibling_items
        prompt_rows = prompt_key_value[group_index]
        prompt_count = prompt_len[group_index]
        table_entries = jnp.concatenate([prompt_rows, cache_rows], axis=0).astype(jnp.float32)
        key_row_block = table_entries[:, 0].reshape(PROMPT_TOKENS + SUFFIX_TOKENS, KEY_VALUE_HEADS, HEAD_SIZE)
        value_row_block = table_entries[:, 1].reshape(PROMPT_TOKENS + SUFFIX_TOKENS, KEY_VALUE_HEADS, HEAD_SIZE)
        query_head_count = query_row_block.astype(jnp.float32).reshape(DECODE_STEPS, KEY_VALUE_HEADS, group_members, HEAD_SIZE)
        scores = jnp.einsum('tkgd,pkd->tkgp', query_head_count, key_row_block, precision=lax.Precision.HIGHEST) / math.sqrt(HEAD_SIZE)
        prompt_seen = jnp.arange(PROMPT_TOKENS, dtype=jnp.int32) < prompt_count
        horizon = own_length + 1 + jnp.arange(DECODE_STEPS, dtype=jnp.int32)
        suffix_seen = jnp.arange(SUFFIX_TOKENS, dtype=jnp.int32)[None, :] < horizon[:, None]
        visible = jnp.concatenate([jnp.broadcast_to(prompt_seen[None, :], (DECODE_STEPS, PROMPT_TOKENS)), suffix_seen], axis=1)
        visible = visible[:, None, None, :]
        scores = jnp.where(visible, scores, masked_score)
        row_max = lax.optimization_barrier(jnp.max(scores, axis=-1, keepdims=True))
        weights = jnp.where(visible, jnp.exp(scores - row_max), 0.0)
        denominator = lax.optimization_barrier(jnp.sum(weights, axis=-1))
        rounded = lax.optimization_barrier(weights.astype(jnp.bfloat16)).astype(jnp.float32)
        weighted = jnp.einsum('tkgp,pkd->tkgd', rounded, value_row_block, precision=lax.Precision.HIGHEST)
        decode_result = weighted / denominator[..., None]
        return decode_result.reshape(DECODE_STEPS, QUERY_HEADS * HEAD_SIZE).astype(jnp.bfloat16)
    attended = lax.map(attend_one, (queries, suffix_cache, sibling_group, suffix_len))
    placing = jnp.zeros((SIBLING_TOTAL,), jnp.int32).at[new_position].set(jnp.arange(SIBLING_TOTAL, dtype=jnp.int32))
    placed = attended[placing]
    flattened = placed.transpose(1, 0, 2).reshape(DECODE_STEPS * SIBLING_TOTAL, QUERY_HEADS * HEAD_SIZE)
    block_output = jnp.dot(flattened.astype(jnp.float32), output_weight.astype(jnp.float32), preferred_element_type=jnp.float32, precision=lax.Precision.HIGHEST)
    block_output = block_output.reshape(DECODE_STEPS, SIBLING_TOTAL, D).astype(jnp.bfloat16)
    moved_cache = jnp.zeros_like(suffix_cache).at[new_position].set(suffix_cache)
    return (moved_cache, block_output)
```

```python
import functools
import math

import jax
import jax.numpy as jnp
from jax import lax
from jax.experimental import pallas as pl
from jax.experimental.pallas import tpu as pltpu
from jax.sharding import PartitionSpec as P

MESH = pl.DeviceIdType.MESH
BF16, F32, I32 = jnp.bfloat16, jnp.float32, jnp.int32
HEAD = 128
X, Z, T = 4, 16, 8
S = 32
UNITS = 16
LANE_UNITS = UNITS // X
CAPACITIES = (28, 64)
masked_score = -1e30

VM = pl.BlockSpec(memory_space=pltpu.VMEM)
SM = pl.BlockSpec(memory_space=pltpu.SMEM)


def place():
    r = lax.axis_index("replica")
    return r // X, lax.rem(r, X), lax.axis_index("tensor")


def to_replica(z, x):
    return dict(device_id={"replica": z * X + x}, device_id_type=MESH)


def to_tensor(t):
    return dict(device_id={"tensor": t}, device_id_type=MESH)


def attend_kernel(
    page_ref, len_ref, slot_ref, group_ref, plen_ref,
    facts_ref, pool_ref, query_ref, fresh_ref, prompt_ref, weight_ref,
    all_facts_ref, xbuf_ref, gathered_ref, wide_ref,
    cache, split, heads, fresh32, f_send, f_recv, g_send, g_recv,
    x_send, x_recv, w_send, w_recv, r_send, r_recv, l_send, l_recv, own_sem,
):
    z, x, _ = place()
    up, down = lax.rem(z + 1, Z), lax.rem(z + Z - 1, Z)
    barrier = pltpu.get_barrier_semaphore()
    for i in range(1, X):
        pl.semaphore_signal(barrier, inc=1, **to_replica(z, lax.rem(x + i, X)))

    @pl.loop(1, Z)
    def _(i):
        pl.semaphore_signal(barrier, inc=1, **to_replica(lax.rem(z + i, Z), x))

    mine = all_facts_ref.at[z, pl.ds(x, 1)]
    all_facts_ref[z, pl.ds(x, 1)] = facts_ref[...]
    pl.semaphore_wait(barrier, X + Z - 2)

    def f_copy(i):
        return pltpu.make_async_remote_copy(
            mine, mine, f_send.at[i], f_recv.at[i], **to_replica(z, lax.rem(x + i, X))
        )

    def g_copy(i):
        return pltpu.make_async_remote_copy(
            all_facts_ref.at[z], all_facts_ref.at[z], g_send.at[i], g_recv.at[i], **to_replica(lax.rem(z + i, Z), x)
        )

    for i in range(1, X):
        f_copy(i).start()

    fresh32[...] = fresh_ref[...].astype(F32)
    row = lax.broadcasted_iota(I32, (16, HEAD), 0)
    odd = lax.rem(row, 2) == 1
    token_of_row = row // 2

    @pl.loop(0, S)
    def _(s):
        length = len_ref[s]
        one = jnp.where(odd, fresh32[pl.ds(4 * s + 1, 1), :], fresh32[pl.ds(4 * s, 1), :])
        two = jnp.where(odd, fresh32[pl.ds(4 * s + 3, 1), :], fresh32[pl.ds(4 * s + 2, 1), :])
        for page in range(8):
            source = page_ref[s * 8 + page]
            for half in range(2):
                unit = pool_ref[source, 16 * half : 16 * (half + 1), :].astype(F32)
                token = token_of_row + (16 * page + 8 * half) - length
                unit = jnp.where(
                    token < 0, unit, jnp.where(token == 0, one, jnp.where(token == 1, two, 0.0))
                )
                cache[s, 2 * page + half] = unit.astype(BF16)

    @pl.loop(0, S)
    def _(s):
        slot = slot_ref[s]
        for lane in range(X):
            turn = lax.rem(lane + 4 * S - lax.rem(slot, 4), 4)
            for k in range(LANE_UNITS):
                split[lane, s, k] = cache[s, 4 * k + turn]

    def x_copy(i):
        lane = lax.rem(x + i, X)
        return pltpu.make_async_remote_copy(
            split.at[lane], xbuf_ref.at[x], x_send.at[i], x_recv.at[i], **to_replica(z, lane)
        )

    def w_copy(i):
        return pltpu.make_async_remote_copy(
            weight_ref, wide_ref.at[x], w_send.at[i], w_recv.at[i], **to_replica(z, lax.rem(x + i, X))
        )

    for i in range(1, X):
        x_copy(i).start()
    for i in range(1, X):
        w_copy(i).start()
    own_split = pltpu.make_async_copy(split.at[x], xbuf_ref.at[x], own_sem.at[0])
    own_weight = pltpu.make_async_copy(weight_ref, wide_ref.at[x], own_sem.at[1])
    own_split.start()
    own_weight.start()
    for i in range(1, X):
        f_copy(i).wait()

    @pl.loop(1, Z)
    def _(i):
        g_copy(i).start()

    scale = 1.0 / math.sqrt(HEAD)
    column = lax.broadcasted_iota(I32, (16, 256), 1)
    step = lax.rem(lax.broadcasted_iota(I32, (16, 256), 0), 2)
    suffix_token = column // 2 - 1 - step
    is_key = lax.rem(column, 2) == 0
    pcolumn = lax.broadcasted_iota(I32, (16, HEAD), 1)
    is_pkey = lax.rem(pcolumn, 2) == 0
    by_column = (((1,), (1,)), ((), ()))

    def attend(s):
        query = query_ref[s]
        group = lax.rem(group_ref[s], 2)
        prompt = prompt_ref[group]
        entries = cache[s].reshape(256, HEAD)
        seen = is_key & (suffix_token < len_ref[s])
        pseen = is_pkey & (pcolumn // 2 < plen_ref[group])
        scores = lax.dot_general(query, entries, by_column, preferred_element_type=F32) * scale
        pscores = lax.dot_general(query, prompt, by_column, preferred_element_type=F32) * scale
        scores = jnp.where(seen, scores, masked_score)
        pscores = jnp.where(pseen, pscores, masked_score)
        top = jnp.maximum(
            jnp.max(scores, axis=1, keepdims=True), jnp.max(pscores, axis=1, keepdims=True)
        )
        weights = jnp.where(seen, jnp.exp(scores - top), 0.0)
        pweights = jnp.where(pseen, jnp.exp(pscores - top), 0.0)
        total = jnp.sum(weights, axis=1, keepdims=True) + jnp.sum(pweights, axis=1, keepdims=True)
        weights = pltpu.roll(weights, 1, 1).astype(BF16)
        pweights = pltpu.roll(pweights, 1, 1).astype(BF16)
        out = jnp.dot(weights, entries, preferred_element_type=F32)
        out = out + jnp.dot(pweights, prompt, preferred_element_type=F32)
        return out / total

    @pl.loop(0, S // 4)
    def _(block):
        outs = [attend(4 * block + i) for i in range(4)]
        for i, out in enumerate(outs):
            for head in range(8):
                for k in range(2):
                    heads[head, pl.ds(k * S + 4 * block + i, 1), :] = out[2 * head + k : 2 * head + k + 1]

    gathered_ref[z] = heads[...].astype(BF16)

    def ring(step, part, forward):
        plane = lax.rem(z + Z - step, Z) if forward else lax.rem(z + step, Z)
        block = gathered_ref.at[plane, pl.ds(4 * part, 4)]
        send, recv = (r_send, r_recv) if forward else (l_send, l_recv)
        return pltpu.make_async_remote_copy(
            block, block, send.at[2 * step + part], recv.at[2 * step + part],
            **to_replica(up if forward else down, x),
        )

    for step in range(Z // 2):
        for part in range(2):
            for forward in (True, False):
                if not forward and step == Z // 2 - 1:
                    continue
                if step:
                    ring(step - 1, part, forward).wait_recv()
                ring(step, part, forward).start()
    for part in range(2):
        ring(Z // 2 - 1, part, True).wait_recv()
        ring(Z // 2 - 2, part, False).wait_recv()
    for step in range(Z // 2):
        for part in range(2):
            for forward in (True, False):
                if not forward and step == Z // 2 - 1:
                    continue
                ring(step, part, forward).wait_send()

    @pl.loop(1, Z)
    def _(i):
        g_copy(i).wait()

    for i in range(1, X):
        w_copy(i).wait()
    for i in range(1, X):
        x_copy(i).wait()
    own_split.wait()
    own_weight.wait()


def attend_call(pages, length, slot, group, plen, facts, pool, query, fresh, prompt, weight):
    half = Z // 2
    return pl.pallas_call(
        attend_kernel,
        out_shape=(
            jax.ShapeDtypeStruct((Z, X, 1, HEAD), I32),
            jax.ShapeDtypeStruct((X, S, LANE_UNITS, 16, HEAD), BF16),
            jax.ShapeDtypeStruct((Z, 8, 2 * S, HEAD), BF16),
            jax.ShapeDtypeStruct((X,) + weight.shape, BF16),
        ),
        in_specs=[SM] * 5 + [VM] * 6,
        out_specs=(VM, VM, VM, VM),
        scratch_shapes=[
            pltpu.VMEM((S, UNITS, 16, HEAD), BF16),
            pltpu.VMEM((X, S, LANE_UNITS, 16, HEAD), BF16),
            pltpu.VMEM((8, 2 * S, HEAD), F32),
            pltpu.VMEM((4 * S, HEAD), F32),
            pltpu.SemaphoreType.DMA((X,)),
            pltpu.SemaphoreType.DMA((X,)),
            pltpu.SemaphoreType.DMA((Z,)),
            pltpu.SemaphoreType.DMA((Z,)),
            pltpu.SemaphoreType.DMA((X,)),
            pltpu.SemaphoreType.DMA((X,)),
            pltpu.SemaphoreType.DMA((X,)),
            pltpu.SemaphoreType.DMA((X,)),
            pltpu.SemaphoreType.DMA((2 * half,)),
            pltpu.SemaphoreType.DMA((2 * half,)),
            pltpu.SemaphoreType.DMA((2 * half,)),
            pltpu.SemaphoreType.DMA((2 * half,)),
            pltpu.SemaphoreType.DMA((2,)),
        ],
        compiler_params=pltpu.CompilerParams(
            collective_id=1, has_side_effects=True, vmem_limit_bytes=40 << 20
        ),
        name="attend_and_gather",
    )(pages, length, slot, group, plen, facts, pool, query, fresh, prompt, weight)


def move_kernel(
    capacity,
    pack_ref, unpack_ref, position_ref, xbuf_ref, gathered_ref, wide_ref,
    moved_ref, block_ref,
    packed, arrived, product, columns, chunk, chunks, deliver,
    z_send, z_recv, c_send, c_recv, t_send, t_recv, d_send, d_recv, own_sem,
):
    z, x, t = place()
    barrier = pltpu.get_barrier_semaphore()

    @pl.loop(1, Z)
    def _(i):
        pl.semaphore_signal(barrier, inc=1, **to_replica(lax.rem(z + i, Z), x))

    for i in range(1, X):
        pl.semaphore_signal(barrier, inc=1, **to_replica(z, lax.rem(x + i, X)))
    for i in range(1, T):
        pl.semaphore_signal(barrier, inc=1, **to_tensor(lax.rem(t + i, T)))
    pl.semaphore_wait(barrier, Z + X + T - 3)

    def z_copy(i):
        plane = lax.rem(z + i, Z)
        return pltpu.make_async_remote_copy(
            packed.at[plane], arrived.at[z], z_send.at[i], z_recv.at[i], **to_replica(plane, x)
        )

    @pl.loop(0, Z)
    def _(i):
        plane = lax.rem(z + i, Z)
        for c in range(capacity):
            packed[plane, c] = xbuf_ref[pack_ref[plane * capacity + c]]

        @pl.when(i > 0)
        def _():
            z_copy(i).start()

    own_plane = pltpu.make_async_copy(packed.at[z], arrived.at[z], own_sem.at[0])
    own_plane.start()
    arrived[Z, 0] = jnp.zeros((16, HEAD), BF16)

    @pl.loop(0, Z // 4)
    def _(b):
        blocks = gathered_ref[pl.ds(4 * b, 4)]
        rows = jnp.concatenate([blocks[:, h].reshape(8 * S, HEAD) for h in range(8)], axis=1)
        for pair in range(X // 2):
            weight = jnp.concatenate([wide_ref[2 * pair], wide_ref[2 * pair + 1]], axis=1)
            out = jnp.dot(rows, weight, preferred_element_type=F32).astype(BF16)
            out = out.reshape(4, 2, S, 2 * HEAD)
            for i in range(2):
                for k in range(2):
                    part = out[:, k, :, i * HEAD : (i + 1) * HEAD].reshape(4 * S, HEAD)
                    product[2 * pair + i, k, pl.ds(pl.multiple_of(b * 4 * S, 4 * S), 4 * S), :] = part

    def c_copy(i):
        lane = lax.rem(x + i, X)
        return pltpu.make_async_remote_copy(
            product.at[lane], columns.at[x], c_send.at[i], c_recv.at[i], **to_replica(z, lane)
        )

    for i in range(1, X):
        c_copy(i).start()
    own_columns = pltpu.make_async_copy(product.at[x], columns.at[x], own_sem.at[1])
    own_columns.start()
    own_columns.wait()
    for i in range(1, X):
        c_copy(i).wait()

    def t_copy(i):
        other = lax.rem(t + i, T)
        return pltpu.make_async_remote_copy(
            chunk.at[other], chunks.at[t], t_send.at[i], t_recv.at[i], **to_tensor(other)
        )

    @pl.loop(0, T)
    def _(n):
        i = lax.rem(n + 1, T)
        other = lax.rem(t + i, T)
        target = lax.broadcasted_iota(I32, (8 * S, Z * S), 0) + other * (8 * S)
        total = jnp.zeros((8 * S, 2 * HEAD), F32)
        for lane in range(X):
            pick = (position_ref[pl.ds(lane, 1), :] == target).astype(F32).astype(BF16)
            rows = jnp.concatenate([columns[lane, 0], columns[lane, 1]], axis=1)
            total = total + jnp.dot(pick, rows, preferred_element_type=F32)
        for k in range(2):
            chunk[other, k] = total[:, k * HEAD : (k + 1) * HEAD].astype(BF16)

        @pl.when(i > 0)
        def _():
            t_copy(i).start()

    own_chunk = pltpu.make_async_copy(chunk.at[t], chunks.at[t], own_sem.at[2])
    own_chunk.start()
    own_chunk.wait()
    for i in range(1, T):
        t_copy(i).wait()
    for k in range(2):
        total = chunks[0, k].astype(F32)
        for n in range(1, T):
            total = total + chunks[n, k].astype(F32)
        block_ref[k] = total.astype(BF16)

    own_plane.wait()

    @pl.loop(1, Z)
    def _(i):
        z_copy(i).wait()

    flat = arrived.at[...]

    def d_copy(i, turn):
        lane = lax.rem(x + i, X)
        return pltpu.make_async_remote_copy(
            deliver.at[lane, :, turn], moved_ref.at[:, turn, :, lax.rem(x + X - turn, X)],
            d_send.at[i, turn], d_recv.at[i, turn], **to_replica(z, lane),
        )

    def own_deliver(turn):
        return pltpu.make_async_copy(
            deliver.at[x, :, turn], moved_ref.at[:, turn, :, lax.rem(x + X - turn, X)], own_sem.at[turn + 3]
        )

    @pl.loop(0, X)
    def _(n):
        i = lax.rem(n + 1, X)
        lane = lax.rem(x + i, X)

        @pl.loop(0, S // 4)
        def _(s):
            for turn in range(4):
                for k in range(LANE_UNITS):
                    index = unpack_ref[((lane * (S // 4) + s) * 4 + turn) * LANE_UNITS + k]
                    deliver[lane, s, turn, k] = flat[index // capacity, lax.rem(index, capacity)]

        @pl.when(i > 0)
        def _():
            for turn in range(4):
                d_copy(i, turn).start()

    for turn in range(4):
        own_deliver(turn).start()
    for turn in range(4):
        own_deliver(turn).wait()
    for i in range(1, X):
        for turn in range(4):
            d_copy(i, turn).wait()


def move_call(number, capacity, pack, unpack, position, xbuf, gathered, wide):
    dma = pltpu.SemaphoreType.DMA
    return pl.pallas_call(
        functools.partial(move_kernel, capacity),
        out_shape=(
            jax.ShapeDtypeStruct((S // 4, 4, LANE_UNITS, X, 16, HEAD), BF16),
            jax.ShapeDtypeStruct((2, 8 * S, HEAD), BF16),
        ),
        in_specs=[SM, SM, VM, VM, VM, VM],
        out_specs=(VM, VM),
        scratch_shapes=[
            pltpu.VMEM((Z, capacity, 16, HEAD), BF16),
            pltpu.VMEM((Z + 1, capacity, 16, HEAD), BF16),
            pltpu.VMEM((X, 2, Z * S, HEAD), BF16),
            pltpu.VMEM((X, 2, Z * S, HEAD), BF16),
            pltpu.VMEM((T, 2, 8 * S, HEAD), BF16),
            pltpu.VMEM((T, 2, 8 * S, HEAD), BF16),
            pltpu.VMEM((X, S // 4, 4, LANE_UNITS, 16, HEAD), BF16),
            dma((Z,)), dma((Z,)), dma((X,)), dma((X,)), dma((T,)), dma((T,)),
            dma((X, 4)), dma((X, 4)), dma((7,)),
        ],
        compiler_params=pltpu.CompilerParams(
            collective_id=2 + number, has_side_effects=True, vmem_limit_bytes=48 << 20
        ),
        name="move_and_project",
    )(pack, unpack, position, xbuf, gathered, wide)


def body(
    queries, fresh_entries, suffix_page_pool, page_table, suffix_len,
    prompt_key_value, prompt_len, sibling_group, new_position, output_weight,
):
    z, x, _ = place()
    facts = jnp.concatenate([new_position, suffix_len, jnp.zeros((2 * S,), I32)]).reshape(1, 1, HEAD)
    query = queries.reshape(S, 2, 8, HEAD).transpose(0, 2, 1, 3).reshape(S, 16, HEAD)
    facts, xbuf, gathered, wide = attend_call(
        page_table.reshape(-1) - (z * X + x) * (S * 8), suffix_len, new_position, sibling_group, prompt_len, facts,
        suffix_page_pool.reshape(S * 8, 32, HEAD), query, fresh_entries.reshape(4 * S, HEAD),
        prompt_key_value.reshape(2, 2 * 64, HEAD), output_weight,
    )

    position = facts[:, :, 0, :S].reshape(Z, X * S)
    tokens = facts[:, :, 0, S : 2 * S].reshape(Z, X * S) + 2
    plane = position // (X * S)
    filled = (tokens + 7) // 8
    lanes = jnp.arange(X, dtype=I32)
    turn = (lanes[:, None, None] - position[None]) % 4
    counts = (filled[None] - turn + 3) // 4
    planes = jnp.arange(Z, dtype=I32)
    load = jnp.sum(
        jnp.where(plane[None, :, None, :] == planes[None, None, :, None], counts[:, :, None, :], 0), axis=3
    )
    largest = jnp.max(load)
    count = jnp.sum(jnp.where((lanes == x)[:, None, None], counts, 0), axis=0)
    members = jnp.arange(X * S, dtype=I32)
    ahead = (plane[:, :, None] == plane[:, None, :]) & (members[None, None, :] < members[None, :, None])
    offset = jnp.sum(jnp.where(ahead, count[:, None, :], 0), axis=2)

    unit = jnp.arange(LANE_UNITS, dtype=I32)
    own = lambda a: lax.dynamic_index_in_dim(a, z, 0, keepdims=False)
    own_count, own_offset, own_plane = own(count), own(offset), own(plane)
    wanted = z * (X * S) + members
    match = (position.reshape(-1)[None, :] == wanted[:, None])
    find = lambda a: jnp.sum(jnp.where(match, a.reshape(-1)[None, :], 0), axis=1)
    from_plane = find(jnp.broadcast_to(planes[:, None], plane.shape))
    from_offset, from_count = find(offset), find(count)
    by_lane = position.reshape(Z, X, S).transpose(1, 0, 2).reshape(X, Z * S)

    def branch(number, capacity):
        def run(xbuf, gathered, wide):
            spot = own_plane[:, None] * capacity + own_offset[:, None] + unit[None, :]
            spot = jnp.where(unit[None, :] < own_count[:, None], spot, -1).reshape(-1)
            spots = jnp.arange(Z * capacity, dtype=I32)
            pack = jnp.sum(
                jnp.where(spot[None, :] == spots[:, None], jnp.arange(spot.shape[0], dtype=I32)[None, :], 0), axis=1
            )
            start = from_plane * capacity + from_offset
            unpack = jnp.where(
                unit[None, :] < from_count[:, None], start[:, None] + unit[None, :], Z * capacity
            ).reshape(-1)
            return move_call(number, capacity, pack, unpack, by_lane, xbuf, gathered, wide)

        return run

    small = sum((largest > c).astype(I32) for c in CAPACITIES[:-1])
    moved, block = lax.switch(
        small, [branch(n, c) for n, c in enumerate(CAPACITIES)],
        xbuf.reshape(X * S * LANE_UNITS, 16, HEAD), gathered, wide,
    )
    return moved.reshape(S, 128, 2, HEAD), block


def solution(mesh):
    placed = (
        P("replica", None, "tensor"),
        P("replica", None, None, "tensor"),
        P("replica", None, None, "tensor"),
        P("replica", None),
        P("replica"),
        P("replica", None, None, "tensor"),
        P("replica"),
        P("replica"),
        P("replica"),
        P("tensor", "replica"),
    )
    return jax.shard_map(
        body,
        mesh=mesh,
        in_specs=placed,
        out_specs=(P("replica", None, None, "tensor"), P(None, "tensor", "replica")),
        check_vma=False,
    )
```

```python
import functools
import math

import jax
import jax.numpy as jnp
from jax import lax
from jax.experimental import pallas as pl
from jax.experimental.pallas import tpu as pltpu
from jax.sharding import PartitionSpec as P

MESH = pl.DeviceIdType.MESH
BF16, F32, I32 = jnp.bfloat16, jnp.float32, jnp.int32
HEAD = 128
X, Z, T = 4, 16, 8
S = 32
UNITS = 16
LANE_UNITS = UNITS // X
CAPACITIES = ((24, 64), (26, 64), (28, 72), (30, 72), (34, 80), (64, 128))
QUARTER = 8
masked_score = -1e30

VM = pl.BlockSpec(memory_space=pltpu.VMEM)
SM = pl.BlockSpec(memory_space=pltpu.SMEM)
HB = pl.BlockSpec(memory_space=pltpu.HBM)


def place():
    r = lax.axis_index("replica")
    return r // X, lax.rem(r, X), lax.axis_index("tensor")


def to_replica(z, x):
    return dict(device_id={"replica": z * X + x}, device_id_type=MESH)


def to_tensor(t):
    return dict(device_id={"tensor": t}, device_id_type=MESH)


def attend_kernel(
    facts_ref, own_facts_ref, pool_hbm, query_hbm, fresh_hbm, prompt_hbm,
    all_facts_ref, xbuf_ref, gathered_ref, position_ref, table_ref,
    pool_ref, query_ref, fresh_ref, prompt_ref, cache, split, heads, fresh32, by_plane, offsets, found,
    in_sem, f_send, f_recv, g_send, g_recv, x_send, x_recv, r_send, r_recv, l_send, l_recv, own_sem,
):
    z, x, _ = place()
    up, down = lax.rem(z + 1, Z), lax.rem(z + Z - 1, Z)
    barrier = pltpu.get_barrier_semaphore()
    inputs = [
        pltpu.make_async_copy(a, b, in_sem.at[i])
        for i, (a, b) in enumerate(
            ((fresh_hbm, fresh_ref), (pool_hbm, pool_ref), (query_hbm, query_ref), (prompt_hbm, prompt_ref))
        )
    ]
    for copy in inputs:
        copy.start()
    for i in range(1, X):
        pl.semaphore_signal(barrier, inc=1, **to_replica(z, lax.rem(x + i, X)))

    @pl.loop(1, Z)
    def _(i):
        pl.semaphore_signal(barrier, inc=1, **to_replica(lax.rem(z + i, Z), x))

    page_of = lambda s, i: facts_ref[s * 8 + i]
    slot_of = lambda s: facts_ref[256 + s]
    length_of = lambda s: facts_ref[288 + s]
    group_of = lambda s: facts_ref[320 + s]
    prompt_length_of = lambda group: facts_ref[352 + group]

    mine = all_facts_ref.at[z, pl.ds(x, 1)]
    all_facts_ref[z, pl.ds(x, 1)] = own_facts_ref[...]

    def f_copy(i):
        return pltpu.make_async_remote_copy(
            mine, mine, f_send.at[i], f_recv.at[i], **to_replica(z, lax.rem(x + i, X))
        )

    def g_copy(i):
        return pltpu.make_async_remote_copy(
            all_facts_ref.at[z], all_facts_ref.at[z], g_send.at[i], g_recv.at[i], **to_replica(lax.rem(z + i, Z), x)
        )

    def x_copy(i, quarter):
        lane = lax.rem(x + i, X)
        rows = pl.ds(quarter * QUARTER, QUARTER)
        return pltpu.make_async_remote_copy(
            split.at[lane, rows], xbuf_ref.at[x, rows], x_send.at[i, quarter], x_recv.at[i, quarter],
            **to_replica(z, lane),
        )

    row = lax.broadcasted_iota(I32, (16, HEAD), 0)
    odd = lax.rem(row, 2) == 1
    token_of_row = row // 2

    def build(s):
        length = length_of(s)
        one = jnp.where(odd, fresh32[pl.ds(4 * s + 1, 1), :], fresh32[pl.ds(4 * s, 1), :])
        two = jnp.where(odd, fresh32[pl.ds(4 * s + 3, 1), :], fresh32[pl.ds(4 * s + 2, 1), :])
        for page in range(8):
            source = page_of(s, page)
            for half in range(2):
                unit = pool_ref[source, 16 * half : 16 * (half + 1), :].astype(F32)
                token = token_of_row + (16 * page + 8 * half) - length
                unit = jnp.where(
                    token < 0, unit, jnp.where(token == 0, one, jnp.where(token == 1, two, 0.0))
                )
                cache[s, 2 * page + half] = unit.astype(BF16)

    def divide(s):
        slot = slot_of(s)
        for lane in range(X):
            turn = lax.rem(lane + 4 * S - lax.rem(slot, 4), 4)
            for k in range(LANE_UNITS):
                split[lane, s, k] = cache[s, 4 * k + turn]

    scale = 1.0 / math.sqrt(HEAD)
    column = lax.broadcasted_iota(I32, (16, 256), 1)
    step = lax.rem(lax.broadcasted_iota(I32, (16, 256), 0), 2)
    suffix_token = column // 2 - 1 - step
    is_key = lax.rem(column, 2) == 0
    pcolumn = lax.broadcasted_iota(I32, (16, HEAD), 1)
    is_pkey = lax.rem(pcolumn, 2) == 0
    by_column = (((1,), (1,)), ((), ()))

    def attend(s):
        query = query_ref[s]
        group = lax.rem(group_of(s), 2)
        prompt = prompt_ref[group]
        entries = cache[s].reshape(256, HEAD)
        seen = is_key & (suffix_token < length_of(s))
        pseen = is_pkey & (pcolumn // 2 < prompt_length_of(group))
        scores = lax.dot_general(query, entries, by_column, preferred_element_type=F32) * scale
        pscores = lax.dot_general(query, prompt, by_column, preferred_element_type=F32) * scale
        scores = jnp.where(seen, scores, masked_score)
        pscores = jnp.where(pseen, pscores, masked_score)
        top = jnp.maximum(
            jnp.max(scores, axis=1, keepdims=True), jnp.max(pscores, axis=1, keepdims=True)
        )
        weights = jnp.where(seen, jnp.exp(scores - top), 0.0)
        pweights = jnp.where(pseen, jnp.exp(pscores - top), 0.0)
        total = jnp.sum(weights, axis=1, keepdims=True) + jnp.sum(pweights, axis=1, keepdims=True)
        weights = pltpu.roll(weights, 1, 1).astype(BF16)
        pweights = pltpu.roll(pweights, 1, 1).astype(BF16)
        out = jnp.dot(weights, entries, preferred_element_type=F32)
        out = out + jnp.dot(pweights, prompt, preferred_element_type=F32)
        return out / total

    def ring(step, part, forward):
        plane = lax.rem(z + Z - step, Z) if forward else lax.rem(z + step, Z)
        block = gathered_ref.at[plane, part]
        send, recv = (r_send, r_recv) if forward else (l_send, l_recv)
        return pltpu.make_async_remote_copy(
            block, block, send.at[2 * step + part], recv.at[2 * step + part],
            **to_replica(up if forward else down, x),
        )

    for copy in inputs[:2]:
        copy.wait()
    fresh32[...] = fresh_ref[...].astype(F32)
    for quarter in range(S // QUARTER):

        @pl.loop(0, QUARTER)
        def _(n):
            build(quarter * QUARTER + n)

        @pl.loop(0, QUARTER)
        def _(n):
            divide(quarter * QUARTER + n)

        if quarter == 0:
            pl.semaphore_wait(barrier, X + Z - 2)
            for i in range(1, X):
                f_copy(i).start()
            for copy in inputs[2:]:
                copy.wait()
        for i in range(1, X):
            x_copy(i, quarter).start()

        @pl.loop(0, QUARTER // 4)
        def _(block):
            first = quarter * QUARTER + 4 * block
            outs = [attend(first + i) for i in range(4)]
            for i, out in enumerate(outs):
                for head in range(8):
                    for k in range(2):
                        place_in = (quarter % 2) * QUARTER + 4 * block + i + k * (S // 2)
                        heads[head, pl.ds(place_in, 1), :] = out[2 * head + k : 2 * head + k + 1]

        if quarter % 2:
            part = quarter // 2
            gathered_ref[z, part] = heads[...].astype(BF16)
            ring(0, part, True).start()
            ring(0, part, False).start()
        if quarter == 1:
            for i in range(1, X):
                f_copy(i).wait()

            @pl.loop(1, Z)
            def _(i):
                g_copy(i).start()

    own_split = pltpu.make_async_copy(split.at[x], xbuf_ref.at[x], own_sem.at[0])
    own_split.start()

    def iota(rows, axis):
        return lax.broadcasted_iota(I32, (rows, HEAD), axis)

    def units_on(lane, slot, filled):
        return (filled - ((lane - slot) & 3) + 3) >> 2

    def pick(a, b):
        return lax.dot_general(a.astype(F32).astype(BF16), b.astype(F32).astype(BF16), by_column, preferred_element_type=F32)

    def gather_facts():
        @pl.loop(1, Z)
        def _(i):
            g_copy(i).wait()

        part = lambda plane, lane: all_facts_ref[plane, lane][:, :S]
        for plane in range(Z):
            by_plane[plane : plane + 1, :] = jnp.concatenate([part(plane, lane) for lane in range(X)], axis=1)
        for lane in range(X):
            row = jnp.concatenate([part(plane, lane) for plane in range(Z)], axis=1)
            position_ref[lane : lane + 1, :] = row >> 7

    def decode(facts):
        return facts >> 7, ((facts & 127) + 9) >> 3

    def pairs():
        position, filled = decode(by_plane[...])
        count = [units_on(lane, position, filled) for lane in range(X)]
        return position, [(count[0] + (count[1] << 12)).astype(F32), (count[2] + (count[3] << 12)).astype(F32)]

    def larger(most, total):
        total = total.astype(I32)
        return jnp.maximum(most, jnp.maximum(total & 4095, total >> 12))

    def find_offsets():
        position, filled = decode(by_plane[...])
        plane = position >> 7
        count = units_on(x, position, filled).astype(F32)
        groups = [plane == i for i in range(Z)]
        stacked = jnp.concatenate([jnp.where(g, count, 0.0) for g in groups], axis=0)
        earlier = (iota(HEAD, 1) < iota(HEAD, 0)).astype(F32)
        sums = pick(stacked, earlier)
        offset = jnp.zeros((Z, HEAD), F32)
        for i, g in enumerate(groups):
            offset = offset + jnp.where(g, sums[i * Z : (i + 1) * Z], 0.0)
        offsets[...] = offset
        mine = iota(Z, 0) == z
        own = lambda a: jnp.sum(jnp.where(mine, a, 0.0), axis=0, keepdims=True)
        own_count, own_offset = own(count), own(offset)
        target = (own(plane.astype(F32)).astype(I32) == iota(Z, 0)).astype(F32)
        ahead = iota(HEAD, 0).astype(F32) - own_offset
        here = ((ahead >= 0.0) & (ahead < own_count)).astype(F32)
        sibling = pick(target * iota(Z, 1).astype(F32), here)
        unit = pick(target, here * ahead)
        table_ref[0:Z, :] = (4.0 * sibling + unit).astype(I32)

    def find_sources():
        wanted = iota(HEAD, 0) + z * (X * S)
        row = iota(8, 0)
        total = jnp.zeros((8, HEAD), F32)
        for plane in range(Z):
            position, filled = decode(by_plane[plane : plane + 1, :])
            values = jnp.where(row == 0, float(plane), jnp.where(row == 1, offsets[plane : plane + 1, :], filled.astype(F32)))
            total = total + pick(values, (position == wanted).astype(F32))
        found[...] = total

    def find_deliveries():
        plane, offset, filled = found[0:1, :], found[1:2, :], found[2:3, :].astype(I32)
        slot, row = iota(1, 1) & (S - 1), iota(8, 0)
        comes = [units_on(lane, slot, filled).astype(F32) for lane in range(X)]
        leaves = units_on(x, slot, filled).astype(F32)
        stacked = jnp.broadcast_to(leaves, (8, HEAD))
        for lane in range(X):
            stacked = jnp.where(row == lane, comes[lane], stacked)
        near = (iota(HEAD, 1) < iota(HEAD, 0)) & ((iota(HEAD, 1) >> 5) == (iota(HEAD, 0) >> 5))
        sums = pick(stacked, near.astype(F32))
        ahead = iota(HEAD, 0).astype(F32) - sums[4:5]
        here = ((ahead >= 0.0) & (ahead < leaves)).astype(F32)
        target = ((iota(8, 1) >> 5) == row).astype(F32)
        spot = 64.0 * pick(target * plane, here) + pick(target * (offset - sums[4:5]), here)
        table_ref[16:24, :] = (spot + pick(target, here) * iota(8, 1).astype(F32)).astype(I32)
        for j in range(X):
            lane = (slot + j) & 3
            first, count = jnp.zeros((1, HEAD), F32), jnp.zeros((1, HEAD), F32)
            for i in range(X):
                first = first + jnp.where(lane == i, sums[i : i + 1] + 128.0 * i, 0.0)
                count = count + jnp.where(lane == i, comes[i], 0.0)
            for k in range(LANE_UNITS):
                value = jnp.where(count > float(k), first + float(k), 128.0 * X)
                table_ref[24 + 4 * k + j : 25 + 4 * k + j, :] = value.astype(I32)

    def find_largest():
        position, counts = pairs()
        largest = jnp.zeros((Z, 1), I32)
        for plane in range(Z):
            for count in counts:
                largest = larger(largest, jnp.sum(jnp.where((position >> 7) == plane, count, 0.0), axis=1, keepdims=True))
        largest = jnp.max(largest.astype(F32), axis=0, keepdims=True).astype(I32)
        table_ref[40:41, :] = jnp.broadcast_to(largest, (1, HEAD))

    def find_most():
        position, counts = pairs()

        def one(replica, most):
            here = (position >> 5) == replica
            for count in counts:
                total = jnp.sum(jnp.sum(jnp.where(here, count, 0.0), axis=0, keepdims=True), axis=1, keepdims=True)
                most = larger(most, total)
            return most

        most = lax.fori_loop(0, Z * X, one, jnp.zeros((1, 1), I32))
        largest = table_ref[40:41, :]
        choice = jnp.zeros((1, HEAD), I32)
        for units, delivered in CAPACITIES[:-1]:
            choice = choice + ((largest > units) | (most > delivered)).astype(I32)
        table_ref[41:48, :] = jnp.broadcast_to(choice, (7, HEAD))

    between = [None, gather_facts, find_offsets, find_sources, find_deliveries, find_largest, find_most, None]

    for step in range(1, Z // 2):
        for part in range(2):
            for forward in (True, False):
                if not forward and step == Z // 2 - 1:
                    continue
                ring(step - 1, part, forward).wait_recv()
                ring(step, part, forward).start()
        if between[step]:
            between[step]()
    for part in range(2):
        ring(Z // 2 - 1, part, True).wait_recv()
        ring(Z // 2 - 2, part, False).wait_recv()
    for step in range(Z // 2):
        for part in range(2):
            for forward in (True, False):
                if not forward and step == Z // 2 - 1:
                    continue
                ring(step, part, forward).wait_send()

    for i in range(1, X):
        for quarter in range(S // QUARTER):
            x_copy(i, quarter).wait()
    own_split.wait()


def attend_call(facts, own_facts, pool, query, fresh, prompt):
    dma = pltpu.SemaphoreType.DMA
    return pl.pallas_call(
        attend_kernel,
        out_shape=(
            jax.ShapeDtypeStruct((Z, X, 1, HEAD), I32),
            jax.ShapeDtypeStruct((X, S, LANE_UNITS, 16, HEAD), BF16),
            jax.ShapeDtypeStruct((Z, 2, 8, S, HEAD), BF16),
            jax.ShapeDtypeStruct((X, Z * S), I32),
            jax.ShapeDtypeStruct((48, HEAD), I32),
        ),
        in_specs=[SM, VM] + [HB] * 4,
        out_specs=(VM,) * 5,
        scratch_shapes=[
            pltpu.VMEM(pool.shape, BF16),
            pltpu.VMEM(query.shape, BF16),
            pltpu.VMEM(fresh.shape, BF16),
            pltpu.VMEM(prompt.shape, BF16),
            pltpu.VMEM((S, UNITS, 16, HEAD), BF16),
            pltpu.VMEM((X, S, LANE_UNITS, 16, HEAD), BF16),
            pltpu.VMEM((8, S, HEAD), F32),
            pltpu.VMEM((4 * S, HEAD), F32),
            pltpu.VMEM((Z, HEAD), I32),
            pltpu.VMEM((Z, HEAD), F32),
            pltpu.VMEM((8, HEAD), F32),
            dma((4,)), dma((X,)), dma((X,)), dma((Z,)), dma((Z,)), dma((X, 4)), dma((X, 4)),
            dma((Z,)), dma((Z,)), dma((Z,)), dma((Z,)), dma((1,)),
        ],
        compiler_params=pltpu.CompilerParams(
            collective_id=1, has_side_effects=True, vmem_limit_bytes=60 << 20
        ),
        name="attend_and_gather",
    )(facts, own_facts, pool, query, fresh, prompt)


def move_kernel(
    capacity, delivery,
    table_ref, position_ref, xbuf_ref, gathered_ref, weight_ref,
    moved_ref, block_ref,
    packed, arrived, wide, product, columns, chunk, chunks, outgoing, incoming,
    z_send, z_recv, w_send, w_recv, c_send, c_recv, t_send, t_recv, d_send, d_recv, own_sem,
):
    z, x, t = place()
    barrier = pltpu.get_barrier_semaphore()

    @pl.loop(1, Z)
    def _(i):
        pl.semaphore_signal(barrier, inc=1, **to_replica(lax.rem(z + i, Z), x))

    for i in range(1, X):
        pl.semaphore_signal(barrier, inc=1, **to_replica(z, lax.rem(x + i, X)))
    for i in range(1, T):
        pl.semaphore_signal(barrier, inc=1, **to_tensor(lax.rem(t + i, T)))
    pl.semaphore_wait(barrier, Z + X + T - 3)

    def z_copy(i):
        plane = lax.rem(z + i, Z)
        return pltpu.make_async_remote_copy(
            packed.at[plane], arrived.at[z], z_send.at[i], z_recv.at[i], **to_replica(plane, x)
        )

    @pl.loop(0, Z)
    def _(i):
        plane = lax.rem(z + i, Z)
        for c in range(capacity):
            packed[plane, c] = xbuf_ref[table_ref[plane, c]]

        @pl.when(i > 0)
        def _():
            z_copy(i).start()

    own_plane = pltpu.make_async_copy(packed.at[z], arrived.at[z], own_sem.at[0])
    own_plane.start()
    incoming[X, 0] = jnp.zeros((16, HEAD), BF16)

    def w_copy(i):
        return pltpu.make_async_remote_copy(
            weight_ref, wide.at[x], w_send.at[i], w_recv.at[i], **to_replica(z, lax.rem(x + i, X))
        )

    for i in range(1, X):
        w_copy(i).start()
    own_weight = pltpu.make_async_copy(weight_ref, wide.at[x], own_sem.at[3])
    own_weight.start()
    own_weight.wait()
    for i in range(1, X):
        w_copy(i).wait()

    @pl.loop(0, Z // 4)
    def _(b):
        blocks = gathered_ref[pl.ds(4 * b, 4)]
        rows = jnp.concatenate([blocks[:, :, h].reshape(8 * S, HEAD) for h in range(8)], axis=1)
        for pair in range(X // 2):
            weight = jnp.concatenate([wide[2 * pair], wide[2 * pair + 1]], axis=1)
            out = jnp.dot(rows, weight, preferred_element_type=F32).astype(BF16)
            out = out.reshape(4, 2, 2, S // 2, 2 * HEAD)
            for i in range(2):
                for k in range(2):
                    part = out[:, :, k, :, i * HEAD : (i + 1) * HEAD].reshape(4 * S, HEAD)
                    product[2 * pair + i, k, pl.ds(pl.multiple_of(b * 4 * S, 4 * S), 4 * S), :] = part

    def c_copy(i):
        lane = lax.rem(x + i, X)
        return pltpu.make_async_remote_copy(
            product.at[lane], columns.at[x], c_send.at[i], c_recv.at[i], **to_replica(z, lane)
        )

    for i in range(1, X):
        c_copy(i).start()
    own_columns = pltpu.make_async_copy(product.at[x], columns.at[x], own_sem.at[1])
    own_columns.start()
    own_columns.wait()
    for i in range(1, X):
        c_copy(i).wait()

    def t_copy(i):
        other = lax.rem(t + i, T)
        return pltpu.make_async_remote_copy(
            chunk.at[other], chunks.at[t], t_send.at[i], t_recv.at[i], **to_tensor(other)
        )

    @pl.loop(0, T)
    def _(n):
        i = lax.rem(n + 1, T)
        other = lax.rem(t + i, T)
        target = lax.broadcasted_iota(I32, (8 * S, Z * S), 0) + other * (8 * S)
        total = jnp.zeros((8 * S, 2 * HEAD), F32)
        for lane in range(X):
            pick = (position_ref[pl.ds(lane, 1), :] == target).astype(F32).astype(BF16)
            rows = jnp.concatenate([columns[lane, 0], columns[lane, 1]], axis=1)
            total = total + jnp.dot(pick, rows, preferred_element_type=F32)
        for k in range(2):
            chunk[other, k] = total[:, k * HEAD : (k + 1) * HEAD].astype(BF16)

        @pl.when(i > 0)
        def _():
            t_copy(i).start()

    own_chunk = pltpu.make_async_copy(chunk.at[t], chunks.at[t], own_sem.at[2])
    own_chunk.start()
    own_chunk.wait()
    for i in range(1, T):
        t_copy(i).wait()
    for k in range(2):
        total = chunks[0, k].astype(F32)
        for n in range(1, T):
            total = total + chunks[n, k].astype(F32)
        block_ref[k] = total.astype(BF16)

    own_plane.wait()

    @pl.loop(1, Z)
    def _(i):
        z_copy(i).wait()

    def d_copy(i):
        lane = lax.rem(x + i, X)
        return pltpu.make_async_remote_copy(
            outgoing.at[lane], incoming.at[x, pl.ds(0, delivery)], d_send.at[i], d_recv.at[i], **to_replica(z, lane)
        )

    @pl.loop(0, X)
    def _(n):
        i = lax.rem(n + 1, X)
        lane = lax.rem(x + i, X)

        @pl.loop(0, delivery // 8)
        def _(c):
            for j in range(8):
                index = table_ref[16 + lane, 8 * c + j]
                outgoing[lane, 8 * c + j] = arrived[index // 64, lax.rem(index, 64)]

        @pl.when(i > 0)
        def _():
            d_copy(i).start()

    own_delivery = pltpu.make_async_copy(outgoing.at[x], incoming.at[x, pl.ds(0, delivery)], own_sem.at[4])
    own_delivery.start()
    own_delivery.wait()
    for i in range(1, X):
        d_copy(i).wait()

    @pl.loop(0, S)
    def _(slot):
        for unit in range(UNITS):
            index = table_ref[24 + unit, x * S + slot]
            moved_ref[slot // 4, lax.rem(slot, 4), unit // 4, unit % 4] = incoming[index // 128, lax.rem(index, 128)]


def move_call(number, capacity, delivery, *operands):
    dma = pltpu.SemaphoreType.DMA
    return pl.pallas_call(
        functools.partial(move_kernel, capacity, delivery),
        out_shape=(
            jax.ShapeDtypeStruct((S // 4, 4, UNITS // 4, 4, 16, HEAD), BF16),
            jax.ShapeDtypeStruct((2, 8 * S, HEAD), BF16),
        ),
        in_specs=[SM, VM, VM, VM, HB],
        out_specs=(VM, VM),
        scratch_shapes=[
            pltpu.VMEM((Z, capacity, 16, HEAD), BF16),
            pltpu.VMEM((Z, capacity, 16, HEAD), BF16),
            pltpu.VMEM((X, 8 * HEAD, HEAD), BF16),
            pltpu.VMEM((X, 2, Z * S, HEAD), BF16),
            pltpu.VMEM((X, 2, Z * S, HEAD), BF16),
            pltpu.VMEM((T, 2, 8 * S, HEAD), BF16),
            pltpu.VMEM((T, 2, 8 * S, HEAD), BF16),
            pltpu.VMEM((X, delivery, 16, HEAD), BF16),
            pltpu.VMEM((X + 1, delivery, 16, HEAD), BF16),
            dma((Z,)), dma((Z,)), dma((X,)), dma((X,)), dma((X,)), dma((X,)), dma((T,)), dma((T,)),
            dma((X,)), dma((X,)), dma((5,)),
        ],
        compiler_params=pltpu.CompilerParams(
            collective_id=2 + number, has_side_effects=True, vmem_limit_bytes=48 << 20
        ),
        name="move_and_project",
    )(*operands)


def body(
    queries, fresh_entries, suffix_page_pool, page_table, suffix_len,
    prompt_key_value, prompt_len, sibling_group, new_position, output_weight,
):
    z, x, _ = place()
    numbers = jnp.concatenate(
        [page_table.reshape(-1) - (z * X + x) * (S * 8), new_position, suffix_len, sibling_group, prompt_len,
         jnp.zeros((30,), I32)]
    )
    own_facts = jnp.pad(new_position * 128 + suffix_len, (0, HEAD - S)).reshape(1, 1, HEAD)
    query = queries.reshape(S, 2, 8, HEAD).transpose(0, 2, 1, 3).reshape(S, 16, HEAD)
    _, xbuf, gathered, position, table = attend_call(
        numbers, own_facts, suffix_page_pool.reshape(S * 8, 32, HEAD), query,
        fresh_entries.reshape(4 * S, HEAD), prompt_key_value.reshape(2, 2 * 64, HEAD),
    )
    moved, block = lax.switch(
        table[41, 0], [functools.partial(move_call, n, c, d) for n, (c, d) in enumerate(CAPACITIES)],
        table, position, xbuf.reshape(X * S * LANE_UNITS, 16, HEAD), gathered, output_weight,
    )
    return moved.reshape(S, 128, 2, HEAD), block


def solution(mesh):
    placed = (
        P("replica", None, "tensor"),
        P("replica", None, None, "tensor"),
        P("replica", None, None, "tensor"),
        P("replica", None),
        P("replica"),
        P("replica", None, None, "tensor"),
        P("replica"),
        P("replica"),
        P("replica"),
        P("tensor", "replica"),
    )
    return jax.shard_map(
        body,
        mesh=mesh,
        in_specs=placed,
        out_specs=(P("replica", None, None, "tensor"), P(None, "tensor", "replica")),
        check_vma=False,
    )
```

```python
import functools
import math

import jax
import jax.numpy as jnp
from jax import lax
from jax.experimental import pallas as pl
from jax.experimental.pallas import tpu as pltpu
from jax.sharding import PartitionSpec as P

MESH = pl.DeviceIdType.MESH
BF16, F32, I32 = jnp.bfloat16, jnp.float32, jnp.int32
HEAD = 128
X, Z, T = 4, 16, 8
S = 32
UNITS = 16
LANE_UNITS = UNITS // X
CAPACITIES = ((24, 64), (26, 64), (28, 72), (30, 72), (34, 80), (64, 128))
QUARTER = 8
QUARTERS = S // QUARTER
FORWARD, BACK = Z // 2, Z // 2 - 1
masked_score = -1e30

VM = pl.BlockSpec(memory_space=pltpu.VMEM)
SM = pl.BlockSpec(memory_space=pltpu.SMEM)
HB = pl.BlockSpec(memory_space=pltpu.HBM)


def place():
    r = lax.axis_index("replica")
    return r // X, lax.rem(r, X), lax.axis_index("tensor")


def to_replica(z, x):
    return dict(device_id={"replica": z * X + x}, device_id_type=MESH)


def to_tensor(t):
    return dict(device_id={"tensor": t}, device_id_type=MESH)


def attend_kernel(
    facts_ref, own_facts_ref, pool_hbm, query_hbm, fresh_hbm, prompt_hbm,
    all_facts_ref, xbuf_ref, gathered_ref, position_ref, table_ref,
    pool_ref, query_ref, fresh_ref, prompt_ref, cache, split, heads, fresh32, by_plane, offsets, found,
    in_sem, f_send, f_recv, g_send, g_recv, x_send, x_recv, r_send, r_recv, l_send, l_recv, own_sem,
):
    z, x, _ = place()
    up, down = lax.rem(z + 1, Z), lax.rem(z + Z - 1, Z)
    barrier = pltpu.get_barrier_semaphore()
    inputs = [
        pltpu.make_async_copy(a, b, in_sem.at[i])
        for i, (a, b) in enumerate(
            ((fresh_hbm, fresh_ref), (pool_hbm, pool_ref), (query_hbm, query_ref), (prompt_hbm, prompt_ref))
        )
    ]
    for copy in inputs:
        copy.start()
    for i in range(1, X):
        pl.semaphore_signal(barrier, inc=1, **to_replica(z, lax.rem(x + i, X)))

    @pl.loop(1, Z)
    def _(i):
        pl.semaphore_signal(barrier, inc=1, **to_replica(lax.rem(z + i, Z), x))

    page_of = lambda s, i: facts_ref[s * 8 + i]
    slot_of = lambda s: facts_ref[256 + s]
    length_of = lambda s: facts_ref[288 + s]
    group_of = lambda s: facts_ref[320 + s]
    prompt_length_of = lambda group: facts_ref[352 + group]

    mine = all_facts_ref.at[z, pl.ds(x, 1)]
    all_facts_ref[z, pl.ds(x, 1)] = own_facts_ref[...]

    def f_copy(i):
        return pltpu.make_async_remote_copy(
            mine, mine, f_send.at[i], f_recv.at[i], **to_replica(z, lax.rem(x + i, X))
        )

    def g_copy(i):
        return pltpu.make_async_remote_copy(
            all_facts_ref.at[z], all_facts_ref.at[z], g_send.at[i], g_recv.at[i], **to_replica(lax.rem(z + i, Z), x)
        )

    def x_copy(i, quarter):
        lane = lax.rem(x + i, X)
        rows = pl.ds(quarter * QUARTER, QUARTER)
        return pltpu.make_async_remote_copy(
            split.at[lane, rows], xbuf_ref.at[x, rows], x_send.at[i, quarter], x_recv.at[i, quarter],
            **to_replica(z, lane),
        )

    row = lax.broadcasted_iota(I32, (16, HEAD), 0)
    odd = lax.rem(row, 2) == 1
    token_of_row = row // 2

    def build(s):
        length = length_of(s)
        one = jnp.where(odd, fresh32[pl.ds(4 * s + 1, 1), :], fresh32[pl.ds(4 * s, 1), :])
        two = jnp.where(odd, fresh32[pl.ds(4 * s + 3, 1), :], fresh32[pl.ds(4 * s + 2, 1), :])
        for page in range(8):
            source = page_of(s, page)
            for half in range(2):
                unit = pool_ref[source, 16 * half : 16 * (half + 1), :].astype(F32)
                token = token_of_row + (16 * page + 8 * half) - length
                unit = jnp.where(
                    token < 0, unit, jnp.where(token == 0, one, jnp.where(token == 1, two, 0.0))
                )
                cache[s, 2 * page + half] = unit.astype(BF16)

    def divide(s):
        slot = slot_of(s)
        for lane in range(X):
            turn = lax.rem(lane + 4 * S - lax.rem(slot, 4), 4)
            for k in range(LANE_UNITS):
                split[lane, s, k] = cache[s, 4 * k + turn]

    scale = 1.0 / math.sqrt(HEAD)
    column = lax.broadcasted_iota(I32, (16, 256), 1)
    step = lax.rem(lax.broadcasted_iota(I32, (16, 256), 0), 2)
    suffix_token = column // 2 - 1 - step
    is_key = lax.rem(column, 2) == 0
    pcolumn = lax.broadcasted_iota(I32, (16, HEAD), 1)
    is_pkey = lax.rem(pcolumn, 2) == 0
    by_column = (((1,), (1,)), ((), ()))

    def attend(s):
        query = query_ref[s]
        group = lax.rem(group_of(s), 2)
        prompt = prompt_ref[group]
        entries = cache[s].reshape(256, HEAD)
        seen = is_key & (suffix_token < length_of(s))
        pseen = is_pkey & (pcolumn // 2 < prompt_length_of(group))
        scores = lax.dot_general(query, entries, by_column, preferred_element_type=F32) * scale
        pscores = lax.dot_general(query, prompt, by_column, preferred_element_type=F32) * scale
        scores = jnp.where(seen, scores, masked_score)
        pscores = jnp.where(pseen, pscores, masked_score)
        top = jnp.maximum(
            jnp.max(scores, axis=1, keepdims=True), jnp.max(pscores, axis=1, keepdims=True)
        )
        weights = jnp.where(seen, jnp.exp(scores - top), 0.0)
        pweights = jnp.where(pseen, jnp.exp(pscores - top), 0.0)
        total = jnp.sum(weights, axis=1, keepdims=True) + jnp.sum(pweights, axis=1, keepdims=True)
        weights = pltpu.roll(weights, 1, 1).astype(BF16)
        pweights = pltpu.roll(pweights, 1, 1).astype(BF16)
        out = jnp.dot(weights, entries, preferred_element_type=F32)
        out = out + jnp.dot(pweights, prompt, preferred_element_type=F32)
        return out / total

    def ring(step, part, forward):
        plane = lax.rem(z + Z - step, Z) if forward else lax.rem(z + step, Z)
        block = gathered_ref.at[plane, part]
        send, recv = (r_send, r_recv) if forward else (l_send, l_recv)
        return pltpu.make_async_remote_copy(
            block, block, send.at[QUARTERS * step + part], recv.at[QUARTERS * step + part],
            **to_replica(up if forward else down, x),
        )

    def turn_ring(wave):
        for part in range(QUARTERS):
            for forward in (True, False):
                if 1 <= wave - part < (FORWARD if forward else BACK):
                    ring(wave - part - 1, part, forward).wait_recv()
                    ring(wave - part, part, forward).start()

    for copy in inputs[:2]:
        copy.wait()
    fresh32[...] = fresh_ref[...].astype(F32)
    for quarter in range(S // QUARTER):

        @pl.loop(0, QUARTER)
        def _(n):
            build(quarter * QUARTER + n)

        @pl.loop(0, QUARTER)
        def _(n):
            divide(quarter * QUARTER + n)

        if quarter == 0:
            pl.semaphore_wait(barrier, X + Z - 2)
            for i in range(1, X):
                f_copy(i).start()
            for copy in inputs[2:]:
                copy.wait()
        for i in range(1, X):
            x_copy(i, quarter).start()

        @pl.loop(0, QUARTER // 4)
        def _(block):
            first = quarter * QUARTER + 4 * block
            outs = [attend(first + i) for i in range(4)]
            for i, out in enumerate(outs):
                for head in range(8):
                    for k in range(2):
                        place_in = 4 * block + i + k * QUARTER
                        heads[head, pl.ds(place_in, 1), :] = out[2 * head + k : 2 * head + k + 1]

        gathered_ref[z, quarter] = heads[...].astype(BF16)
        ring(0, quarter, True).start()
        ring(0, quarter, False).start()
        turn_ring(quarter)
        if quarter == 1:
            for i in range(1, X):
                f_copy(i).wait()

            @pl.loop(1, Z)
            def _(i):
                g_copy(i).start()

    own_split = pltpu.make_async_copy(split.at[x], xbuf_ref.at[x], own_sem.at[0])
    own_split.start()

    def iota(rows, axis):
        return lax.broadcasted_iota(I32, (rows, HEAD), axis)

    def units_on(lane, slot, filled):
        return (filled - ((lane - slot) & 3) + 3) >> 2

    def pick(a, b):
        return lax.dot_general(a.astype(F32).astype(BF16), b.astype(F32).astype(BF16), by_column, preferred_element_type=F32)

    def gather_facts():
        @pl.loop(1, Z)
        def _(i):
            g_copy(i).wait()

        part = lambda plane, lane: all_facts_ref[plane, lane][:, :S]
        for plane in range(Z):
            by_plane[plane : plane + 1, :] = jnp.concatenate([part(plane, lane) for lane in range(X)], axis=1)
        for lane in range(X):
            row = jnp.concatenate([part(plane, lane) for plane in range(Z)], axis=1)
            position_ref[lane : lane + 1, :] = row >> 7

    def decode(facts):
        return facts >> 7, ((facts & 127) + 9) >> 3

    def pairs():
        position, filled = decode(by_plane[...])
        count = [units_on(lane, position, filled) for lane in range(X)]
        return position, [(count[0] + (count[1] << 12)).astype(F32), (count[2] + (count[3] << 12)).astype(F32)]

    def larger(most, total):
        total = total.astype(I32)
        return jnp.maximum(most, jnp.maximum(total & 4095, total >> 12))

    def find_offsets():
        position, filled = decode(by_plane[...])
        plane = position >> 7
        count = units_on(x, position, filled).astype(F32)
        groups = [plane == i for i in range(Z)]
        stacked = jnp.concatenate([jnp.where(g, count, 0.0) for g in groups], axis=0)
        earlier = (iota(HEAD, 1) < iota(HEAD, 0)).astype(F32)
        sums = pick(stacked, earlier)
        offset = jnp.zeros((Z, HEAD), F32)
        for i, g in enumerate(groups):
            offset = offset + jnp.where(g, sums[i * Z : (i + 1) * Z], 0.0)
        offsets[...] = offset
        mine = iota(Z, 0) == z
        own = lambda a: jnp.sum(jnp.where(mine, a, 0.0), axis=0, keepdims=True)
        own_count, own_offset = own(count), own(offset)
        target = (own(plane.astype(F32)).astype(I32) == iota(Z, 0)).astype(F32)
        ahead = iota(HEAD, 0).astype(F32) - own_offset
        here = ((ahead >= 0.0) & (ahead < own_count)).astype(F32)
        sibling = pick(target * iota(Z, 1).astype(F32), here)
        unit = pick(target, here * ahead)
        table_ref[0:Z, :] = (4.0 * sibling + unit).astype(I32)

    def find_sources():
        wanted = iota(HEAD, 0) + z * (X * S)
        row = iota(8, 0)
        total = jnp.zeros((8, HEAD), F32)
        for plane in range(Z):
            position, filled = decode(by_plane[plane : plane + 1, :])
            values = jnp.where(row == 0, float(plane), jnp.where(row == 1, offsets[plane : plane + 1, :], filled.astype(F32)))
            total = total + pick(values, (position == wanted).astype(F32))
        found[...] = total

    def find_deliveries():
        plane, offset, filled = found[0:1, :], found[1:2, :], found[2:3, :].astype(I32)
        slot, row = iota(1, 1) & (S - 1), iota(8, 0)
        comes = [units_on(lane, slot, filled).astype(F32) for lane in range(X)]
        leaves = units_on(x, slot, filled).astype(F32)
        stacked = jnp.broadcast_to(leaves, (8, HEAD))
        for lane in range(X):
            stacked = jnp.where(row == lane, comes[lane], stacked)
        near = (iota(HEAD, 1) < iota(HEAD, 0)) & ((iota(HEAD, 1) >> 5) == (iota(HEAD, 0) >> 5))
        sums = pick(stacked, near.astype(F32))
        ahead = iota(HEAD, 0).astype(F32) - sums[4:5]
        here = ((ahead >= 0.0) & (ahead < leaves)).astype(F32)
        target = ((iota(8, 1) >> 5) == row).astype(F32)
        spot = 64.0 * pick(target * plane, here) + pick(target * (offset - sums[4:5]), here)
        table_ref[16:24, :] = (spot + pick(target, here) * iota(8, 1).astype(F32)).astype(I32)
        for j in range(X):
            lane = (slot + j) & 3
            first, count = jnp.zeros((1, HEAD), F32), jnp.zeros((1, HEAD), F32)
            for i in range(X):
                first = first + jnp.where(lane == i, sums[i : i + 1] + 128.0 * i, 0.0)
                count = count + jnp.where(lane == i, comes[i], 0.0)
            for k in range(LANE_UNITS):
                value = jnp.where(count > float(k), first + float(k), 128.0 * X)
                table_ref[24 + 4 * k + j : 25 + 4 * k + j, :] = value.astype(I32)

    def find_largest():
        position, counts = pairs()
        largest = jnp.zeros((Z, 1), I32)
        for plane in range(Z):
            for count in counts:
                largest = larger(largest, jnp.sum(jnp.where((position >> 7) == plane, count, 0.0), axis=1, keepdims=True))
        largest = jnp.max(largest.astype(F32), axis=0, keepdims=True).astype(I32)
        table_ref[40:41, :] = jnp.broadcast_to(largest, (1, HEAD))

    def find_most():
        position, counts = pairs()

        def one(replica, most):
            here = (position >> 5) == replica
            for count in counts:
                total = jnp.sum(jnp.sum(jnp.where(here, count, 0.0), axis=0, keepdims=True), axis=1, keepdims=True)
                most = larger(most, total)
            return most

        most = lax.fori_loop(0, Z * X, one, jnp.zeros((1, 1), I32))
        largest = table_ref[40:41, :]
        choice = jnp.zeros((1, HEAD), I32)
        for units, delivered in CAPACITIES[:-1]:
            choice = choice + ((largest > units) | (most > delivered)).astype(I32)
        table_ref[41:48, :] = jnp.broadcast_to(choice, (7, HEAD))

    between = [gather_facts, find_offsets, find_sources, find_deliveries, find_largest, find_most]
    for wave in range(QUARTERS, QUARTERS + FORWARD - 1):
        turn_ring(wave)
        if between:
            between.pop(0)()
    for part in range(QUARTERS):
        for forward in (True, False):
            steps = FORWARD if forward else BACK
            ring(steps - 1, part, forward).wait_recv()
            for step in range(steps):
                ring(step, part, forward).wait_send()
    for i in range(1, X):
        for quarter in range(S // QUARTER):
            x_copy(i, quarter).wait()
    own_split.wait()


def attend_call(facts, own_facts, pool, query, fresh, prompt):
    dma = pltpu.SemaphoreType.DMA
    return pl.pallas_call(
        attend_kernel,
        out_shape=(
            jax.ShapeDtypeStruct((Z, X, 1, HEAD), I32),
            jax.ShapeDtypeStruct((X, S, LANE_UNITS, 16, HEAD), BF16),
            jax.ShapeDtypeStruct((Z, QUARTERS, 8, 2 * QUARTER, HEAD), BF16),
            jax.ShapeDtypeStruct((X, Z * S), I32),
            jax.ShapeDtypeStruct((48, HEAD), I32),
        ),
        in_specs=[SM, VM] + [HB] * 4,
        out_specs=(VM,) * 5,
        scratch_shapes=[
            pltpu.VMEM(pool.shape, BF16),
            pltpu.VMEM(query.shape, BF16),
            pltpu.VMEM(fresh.shape, BF16),
            pltpu.VMEM(prompt.shape, BF16),
            pltpu.VMEM((S, UNITS, 16, HEAD), BF16),
            pltpu.VMEM((X, S, LANE_UNITS, 16, HEAD), BF16),
            pltpu.VMEM((8, 2 * QUARTER, HEAD), F32),
            pltpu.VMEM((4 * S, HEAD), F32),
            pltpu.VMEM((Z, HEAD), I32),
            pltpu.VMEM((Z, HEAD), F32),
            pltpu.VMEM((8, HEAD), F32),
            dma((4,)), dma((X,)), dma((X,)), dma((Z,)), dma((Z,)), dma((X, 4)), dma((X, 4)),
            *[dma((QUARTERS * FORWARD,))] * 4, dma((1,)),
        ],
        compiler_params=pltpu.CompilerParams(
            collective_id=1, has_side_effects=True, vmem_limit_bytes=60 << 20
        ),
        name="attend_and_gather",
    )(facts, own_facts, pool, query, fresh, prompt)


def move_kernel(
    capacity, delivery,
    table_ref, position_ref, xbuf_ref, gathered_ref, weight_ref,
    moved_ref, block_ref,
    packed, arrived, wide, product, columns, chunk, chunks, outgoing, incoming,
    z_send, z_recv, w_send, w_recv, c_send, c_recv, t_send, t_recv, d_send, d_recv, own_sem,
):
    z, x, t = place()
    barrier = pltpu.get_barrier_semaphore()

    @pl.loop(1, Z)
    def _(i):
        pl.semaphore_signal(barrier, inc=1, **to_replica(lax.rem(z + i, Z), x))

    for i in range(1, X):
        pl.semaphore_signal(barrier, inc=1, **to_replica(z, lax.rem(x + i, X)))
    for i in range(1, T):
        pl.semaphore_signal(barrier, inc=1, **to_tensor(lax.rem(t + i, T)))
    pl.semaphore_wait(barrier, Z + X + T - 3)

    def z_copy(i):
        plane = lax.rem(z + i, Z)
        return pltpu.make_async_remote_copy(
            packed.at[plane], arrived.at[z], z_send.at[i], z_recv.at[i], **to_replica(plane, x)
        )

    @pl.loop(0, Z)
    def _(i):
        plane = lax.rem(z + i, Z)
        for c in range(capacity):
            packed[plane, c] = xbuf_ref[table_ref[plane, c]]

        @pl.when(i > 0)
        def _():
            z_copy(i).start()

    own_plane = pltpu.make_async_copy(packed.at[z], arrived.at[z], own_sem.at[0])
    own_plane.start()
    incoming[X, 0] = jnp.zeros((16, HEAD), BF16)

    def w_copy(i):
        return pltpu.make_async_remote_copy(
            weight_ref, wide.at[x], w_send.at[i], w_recv.at[i], **to_replica(z, lax.rem(x + i, X))
        )

    for i in range(1, X):
        w_copy(i).start()
    own_weight = pltpu.make_async_copy(weight_ref, wide.at[x], own_sem.at[3])
    own_weight.start()
    own_weight.wait()
    for i in range(1, X):
        w_copy(i).wait()

    def multiply(planes):
        blocks = [block[...] for _, block in planes]
        rows = [jnp.concatenate([b[:, h].reshape(2 * S, HEAD) for b in blocks], axis=0) for h in range(8)]
        rows = jnp.concatenate(rows, axis=1)
        for pair in range(X // 2):
            weight = jnp.concatenate([wide[2 * pair], wide[2 * pair + 1]], axis=1)
            out = jnp.dot(rows, weight, preferred_element_type=F32)
            out = out.reshape(4, QUARTERS, 2, QUARTER, 2 * HEAD)
            for k in range(2):
                part = out[:, :, k].reshape(4, S, 2 * HEAD).astype(BF16)
                for n, (plane, _) in enumerate(planes):
                    target = pl.ds(plane * S, S)
                    for i in range(2):
                        product[2 * pair + i, k, target, :] = part[n, :, i * HEAD : (i + 1) * HEAD]

    for group in range(0, Z, 4):
        multiply([(plane, gathered_ref.at[plane]) for plane in range(group, group + 4)])

    def c_copy(i):
        lane = lax.rem(x + i, X)
        return pltpu.make_async_remote_copy(
            product.at[lane], columns.at[x], c_send.at[i], c_recv.at[i], **to_replica(z, lane)
        )

    for i in range(1, X):
        c_copy(i).start()
    own_columns = pltpu.make_async_copy(product.at[x], columns.at[x], own_sem.at[1])
    own_columns.start()
    own_columns.wait()
    for i in range(1, X):
        c_copy(i).wait()

    def t_copy(i):
        other = lax.rem(t + i, T)
        return pltpu.make_async_remote_copy(
            chunk.at[other], chunks.at[t], t_send.at[i], t_recv.at[i], **to_tensor(other)
        )

    @pl.loop(0, T)
    def _(n):
        i = lax.rem(n + 1, T)
        other = lax.rem(t + i, T)
        target = lax.broadcasted_iota(I32, (8 * S, Z * S), 0) + other * (8 * S)
        total = jnp.zeros((8 * S, 2 * HEAD), F32)
        for lane in range(X):
            pick = (position_ref[pl.ds(lane, 1), :] == target).astype(F32).astype(BF16)
            rows = jnp.concatenate([columns[lane, 0], columns[lane, 1]], axis=1)
            total = total + jnp.dot(pick, rows, preferred_element_type=F32)
        for k in range(2):
            chunk[other, k] = total[:, k * HEAD : (k + 1) * HEAD].astype(BF16)

        @pl.when(i > 0)
        def _():
            t_copy(i).start()

    own_chunk = pltpu.make_async_copy(chunk.at[t], chunks.at[t], own_sem.at[2])
    own_chunk.start()
    own_chunk.wait()
    for i in range(1, T):
        t_copy(i).wait()
    for k in range(2):
        total = chunks[0, k].astype(F32)
        for n in range(1, T):
            total = total + chunks[n, k].astype(F32)
        block_ref[k] = total.astype(BF16)

    own_plane.wait()

    @pl.loop(1, Z)
    def _(i):
        z_copy(i).wait()

    def d_copy(i):
        lane = lax.rem(x + i, X)
        return pltpu.make_async_remote_copy(
            outgoing.at[lane], incoming.at[x, pl.ds(0, delivery)], d_send.at[i], d_recv.at[i], **to_replica(z, lane)
        )

    @pl.loop(0, X)
    def _(n):
        i = lax.rem(n + 1, X)
        lane = lax.rem(x + i, X)

        @pl.loop(0, delivery // 8)
        def _(c):
            for j in range(8):
                index = table_ref[16 + lane, 8 * c + j]
                outgoing[lane, 8 * c + j] = arrived[index // 64, lax.rem(index, 64)]

        @pl.when(i > 0)
        def _():
            d_copy(i).start()

    own_delivery = pltpu.make_async_copy(outgoing.at[x], incoming.at[x, pl.ds(0, delivery)], own_sem.at[4])
    own_delivery.start()
    own_delivery.wait()
    for i in range(1, X):
        d_copy(i).wait()

    @pl.loop(0, S)
    def _(slot):
        for unit in range(UNITS):
            index = table_ref[24 + unit, x * S + slot]
            moved_ref[slot // 4, lax.rem(slot, 4), unit // 4, unit % 4] = incoming[index // 128, lax.rem(index, 128)]


def move_call(number, capacity, delivery, *operands):
    dma = pltpu.SemaphoreType.DMA
    return pl.pallas_call(
        functools.partial(move_kernel, capacity, delivery),
        out_shape=(
            jax.ShapeDtypeStruct((S // 4, 4, UNITS // 4, 4, 16, HEAD), BF16),
            jax.ShapeDtypeStruct((2, 8 * S, HEAD), BF16),
        ),
        in_specs=[SM, VM, VM, VM, HB],
        out_specs=(VM, VM),
        scratch_shapes=[
            pltpu.VMEM((Z, capacity, 16, HEAD), BF16),
            pltpu.VMEM((Z, capacity, 16, HEAD), BF16),
            pltpu.VMEM((X, 8 * HEAD, HEAD), BF16),
            pltpu.VMEM((X, 2, Z * S, HEAD), BF16),
            pltpu.VMEM((X, 2, Z * S, HEAD), BF16),
            pltpu.VMEM((T, 2, 8 * S, HEAD), BF16),
            pltpu.VMEM((T, 2, 8 * S, HEAD), BF16),
            pltpu.VMEM((X, delivery, 16, HEAD), BF16),
            pltpu.VMEM((X + 1, delivery, 16, HEAD), BF16),
            dma((Z,)), dma((Z,)), dma((X,)), dma((X,)), dma((X,)), dma((X,)), dma((T,)), dma((T,)),
            dma((X,)), dma((X,)), dma((5,)),
        ],
        compiler_params=pltpu.CompilerParams(
            collective_id=2 + number, has_side_effects=True, vmem_limit_bytes=48 << 20
        ),
        name="move_and_project",
    )(*operands)


def body(
    queries, fresh_entries, suffix_page_pool, page_table, suffix_len,
    prompt_key_value, prompt_len, sibling_group, new_position, output_weight,
):
    z, x, _ = place()
    numbers = jnp.concatenate(
        [page_table.reshape(-1) - (z * X + x) * (S * 8), new_position, suffix_len, sibling_group, prompt_len,
         jnp.zeros((30,), I32)]
    )
    own_facts = jnp.pad(new_position * 128 + suffix_len, (0, HEAD - S)).reshape(1, 1, HEAD)
    query = queries.reshape(S, 2, 8, HEAD).transpose(0, 2, 1, 3).reshape(S, 16, HEAD)
    _, xbuf, gathered, position, table = attend_call(
        numbers, own_facts, suffix_page_pool.reshape(S * 8, 32, HEAD), query,
        fresh_entries.reshape(4 * S, HEAD), prompt_key_value.reshape(2, 2 * 64, HEAD),
    )
    moved, block = lax.switch(
        table[41, 0], [functools.partial(move_call, n, c, d) for n, (c, d) in enumerate(CAPACITIES)],
        table, position, xbuf.reshape(X * S * LANE_UNITS, 16, HEAD), gathered, output_weight,
    )
    return moved.reshape(S, 128, 2, HEAD), block


def solution(mesh):
    placed = (
        P("replica", None, "tensor"),
        P("replica", None, None, "tensor"),
        P("replica", None, None, "tensor"),
        P("replica", None),
        P("replica"),
        P("replica", None, None, "tensor"),
        P("replica"),
        P("replica"),
        P("replica"),
        P("tensor", "replica"),
    )
    return jax.shard_map(
        body,
        mesh=mesh,
        in_specs=placed,
        out_specs=(P("replica", None, None, "tensor"), P(None, "tensor", "replica")),
        check_vma=False,
    )
```

```python
import functools
import math

import jax
import jax.numpy as jnp
from jax import lax
from jax.experimental import pallas as pl
from jax.experimental.pallas import tpu as pltpu
from jax.sharding import PartitionSpec as P

MESH = pl.DeviceIdType.MESH
BF16, F32, I32 = jnp.bfloat16, jnp.float32, jnp.int32
HEAD = 128
X, Z, T = 4, 16, 8
S = 32
UNITS = 16
LANE_UNITS = UNITS // X
CAPACITIES = ((24, 64), (26, 64), (28, 72), (30, 72), (34, 80), (64, 128))
QUARTER = 8
QUARTERS = S // QUARTER
FORWARD, BACK = Z // 2, Z // 2 - 1
masked_score = -1e30

VM = pl.BlockSpec(memory_space=pltpu.VMEM)
SM = pl.BlockSpec(memory_space=pltpu.SMEM)
HB = pl.BlockSpec(memory_space=pltpu.HBM)


def place():
    r = lax.axis_index("replica")
    return r // X, lax.rem(r, X), lax.axis_index("tensor")


def to_replica(z, x):
    return dict(device_id={"replica": z * X + x}, device_id_type=MESH)


def to_tensor(t):
    return dict(device_id={"tensor": t}, device_id_type=MESH)


def attend_kernel(
    facts_ref, own_facts_ref, pool_hbm, query_hbm, fresh_hbm, prompt_hbm,
    all_facts_ref, xbuf_ref, gathered_ref, position_ref, table_ref,
    pool_ref, query_ref, fresh_ref, prompt_ref, cache, split, heads, fresh32, by_plane, offsets, found,
    in_sem, f_send, f_recv, g_send, g_recv, x_send, x_recv, r_send, r_recv, l_send, l_recv, own_sem,
):
    z, x, _ = place()
    up, down = lax.rem(z + 1, Z), lax.rem(z + Z - 1, Z)
    barrier = pltpu.get_barrier_semaphore()
    inputs = [
        pltpu.make_async_copy(a, b, in_sem.at[i])
        for i, (a, b) in enumerate(
            ((fresh_hbm, fresh_ref), (pool_hbm, pool_ref), (query_hbm, query_ref), (prompt_hbm, prompt_ref))
        )
    ]
    for copy in inputs:
        copy.start()
    for i in range(1, X):
        pl.semaphore_signal(barrier, inc=1, **to_replica(z, lax.rem(x + i, X)))

    @pl.loop(1, Z)
    def _(i):
        pl.semaphore_signal(barrier, inc=1, **to_replica(lax.rem(z + i, Z), x))

    page_of = lambda s, i: facts_ref[i * S + s]
    slot_of = lambda s: facts_ref[256 + s]
    length_of = lambda s: facts_ref[288 + s]
    group_of = lambda s: facts_ref[320 + s]
    prompt_length_of = lambda group: facts_ref[352 + group]

    mine = all_facts_ref.at[z, pl.ds(x, 1)]
    all_facts_ref[z, pl.ds(x, 1)] = own_facts_ref[...]

    def f_copy(i):
        return pltpu.make_async_remote_copy(
            mine, mine, f_send.at[i], f_recv.at[i], **to_replica(z, lax.rem(x + i, X))
        )

    def g_copy(i):
        return pltpu.make_async_remote_copy(
            all_facts_ref.at[z], all_facts_ref.at[z], g_send.at[i], g_recv.at[i], **to_replica(lax.rem(z + i, Z), x)
        )

    def x_copy(i, quarter):
        lane = lax.rem(x + i, X)
        rows = pl.ds(quarter * QUARTER, QUARTER)
        return pltpu.make_async_remote_copy(
            split.at[lane, rows], xbuf_ref.at[x, rows], x_send.at[i, quarter], x_recv.at[i, quarter],
            **to_replica(z, lane),
        )

    row = lax.broadcasted_iota(I32, (16, HEAD), 0)
    odd = lax.rem(row, 2) == 1
    token_of_row = row // 2

    def build(s):
        length = length_of(s)
        one = jnp.where(odd, fresh32[pl.ds(4 * s + 1, 1), :], fresh32[pl.ds(4 * s, 1), :])
        two = jnp.where(odd, fresh32[pl.ds(4 * s + 3, 1), :], fresh32[pl.ds(4 * s + 2, 1), :])
        for page in range(8):
            source = page_of(s, page)
            for half in range(2):
                unit = pool_ref[source, 16 * half : 16 * (half + 1), :].astype(F32)
                token = token_of_row + (16 * page + 8 * half) - length
                unit = jnp.where(
                    token < 0, unit, jnp.where(token == 0, one, jnp.where(token == 1, two, 0.0))
                )
                cache[s, 2 * page + half] = unit.astype(BF16)

    def divide(s):
        slot = slot_of(s)
        for lane in range(X):
            turn = lax.rem(lane + 4 * S - lax.rem(slot, 4), 4)
            for k in range(LANE_UNITS):
                split[lane, s, k] = cache[s, 4 * k + turn]

    scale = 1.0 / math.sqrt(HEAD)
    column = lax.broadcasted_iota(I32, (16, 256), 1)
    step = lax.rem(lax.broadcasted_iota(I32, (16, 256), 0), 2)
    suffix_token = column // 2 - 1 - step
    is_key = lax.rem(column, 2) == 0
    pcolumn = lax.broadcasted_iota(I32, (16, HEAD), 1)
    is_pkey = lax.rem(pcolumn, 2) == 0
    by_column = (((1,), (1,)), ((), ()))

    def attend(s):
        query = query_ref[s]
        group = lax.rem(group_of(s), 2)
        prompt = prompt_ref[group]
        entries = cache[s].reshape(256, HEAD)
        seen = is_key & (suffix_token < length_of(s))
        pseen = is_pkey & (pcolumn // 2 < prompt_length_of(group))
        scores = lax.dot_general(query, entries, by_column, preferred_element_type=F32) * scale
        pscores = lax.dot_general(query, prompt, by_column, preferred_element_type=F32) * scale
        scores = jnp.where(seen, scores, masked_score)
        pscores = jnp.where(pseen, pscores, masked_score)
        top = jnp.maximum(
            jnp.max(scores, axis=1, keepdims=True), jnp.max(pscores, axis=1, keepdims=True)
        )
        weights = jnp.where(seen, jnp.exp(scores - top), 0.0)
        pweights = jnp.where(pseen, jnp.exp(pscores - top), 0.0)
        total = jnp.sum(weights, axis=1, keepdims=True) + jnp.sum(pweights, axis=1, keepdims=True)
        weights = pltpu.roll(weights, 1, 1).astype(BF16)
        pweights = pltpu.roll(pweights, 1, 1).astype(BF16)
        out = jnp.dot(weights, entries, preferred_element_type=F32)
        out = out + jnp.dot(pweights, prompt, preferred_element_type=F32)
        return out / total

    def ring(step, part, forward):
        plane = lax.rem(z + Z - step, Z) if forward else lax.rem(z + step, Z)
        block = gathered_ref.at[plane, part]
        send, recv = (r_send, r_recv) if forward else (l_send, l_recv)
        return pltpu.make_async_remote_copy(
            block, block, send.at[QUARTERS * step + part], recv.at[QUARTERS * step + part],
            **to_replica(up if forward else down, x),
        )

    def turn_ring(wave):
        for part in range(QUARTERS):
            for forward in (True, False):
                if 1 <= wave - part < (FORWARD if forward else BACK):
                    ring(wave - part - 1, part, forward).wait_recv()
                    ring(wave - part, part, forward).start()

    for copy in inputs[:2]:
        copy.wait()
    fresh32[...] = fresh_ref[...].astype(F32)
    for quarter in range(S // QUARTER):

        @pl.loop(0, QUARTER)
        def _(n):
            build(quarter * QUARTER + n)

        @pl.loop(0, QUARTER)
        def _(n):
            divide(quarter * QUARTER + n)

        if quarter == 0:
            pl.semaphore_wait(barrier, X + Z - 2)
            for i in range(1, X):
                f_copy(i).start()
            for copy in inputs[2:]:
                copy.wait()
        for i in range(1, X):
            x_copy(i, quarter).start()

        @pl.loop(0, QUARTER // 4)
        def _(block):
            first = quarter * QUARTER + 4 * block
            outs = [attend(first + i) for i in range(4)]
            for i, out in enumerate(outs):
                for head in range(8):
                    for k in range(2):
                        place_in = 4 * block + i + k * QUARTER
                        heads[head, pl.ds(place_in, 1), :] = out[2 * head + k : 2 * head + k + 1]

        gathered_ref[z, quarter] = heads[...].astype(BF16)
        ring(0, quarter, True).start()
        ring(0, quarter, False).start()
        turn_ring(quarter)
        if quarter == 1:
            for i in range(1, X):
                f_copy(i).wait()

            @pl.loop(1, Z)
            def _(i):
                g_copy(i).start()

    own_split = pltpu.make_async_copy(split.at[x], xbuf_ref.at[x], own_sem.at[0])
    own_split.start()

    def iota(rows, axis):
        return lax.broadcasted_iota(I32, (rows, HEAD), axis)

    def units_on(lane, slot, filled):
        return (filled - ((lane - slot) & 3) + 3) >> 2

    def pick(a, b):
        return lax.dot_general(a.astype(F32).astype(BF16), b.astype(F32).astype(BF16), by_column, preferred_element_type=F32)

    def gather_facts():
        @pl.loop(1, Z)
        def _(i):
            g_copy(i).wait()

        part = lambda plane, lane: all_facts_ref[plane, lane][:, :S]
        for plane in range(Z):
            by_plane[plane : plane + 1, :] = jnp.concatenate([part(plane, lane) for lane in range(X)], axis=1)
        for lane in range(X):
            row = jnp.concatenate([part(plane, lane) for plane in range(Z)], axis=1)
            position_ref[lane : lane + 1, :] = row >> 7

    def decode(facts):
        return facts >> 7, ((facts & 127) + 9) >> 3

    def pairs():
        position, filled = decode(by_plane[...])
        count = [units_on(lane, position, filled) for lane in range(X)]
        return position, [(count[0] + (count[1] << 12)).astype(F32), (count[2] + (count[3] << 12)).astype(F32)]

    def larger(most, total):
        total = total.astype(I32)
        return jnp.maximum(most, jnp.maximum(total & 4095, total >> 12))

    def find_offsets():
        position, filled = decode(by_plane[...])
        plane = position >> 7
        count = units_on(x, position, filled).astype(F32)
        groups = [plane == i for i in range(Z)]
        stacked = jnp.concatenate([jnp.where(g, count, 0.0) for g in groups], axis=0)
        earlier = (iota(HEAD, 1) < iota(HEAD, 0)).astype(F32)
        sums = pick(stacked, earlier)
        offset = jnp.zeros((Z, HEAD), F32)
        for i, g in enumerate(groups):
            offset = offset + jnp.where(g, sums[i * Z : (i + 1) * Z], 0.0)
        offsets[...] = offset
        mine = iota(Z, 0) == z
        own = lambda a: jnp.sum(jnp.where(mine, a, 0.0), axis=0, keepdims=True)
        own_count, own_offset = own(count), own(offset)
        target = (own(plane.astype(F32)).astype(I32) == iota(Z, 0)).astype(F32)
        ahead = iota(HEAD, 0).astype(F32) - own_offset
        here = ((ahead >= 0.0) & (ahead < own_count)).astype(F32)
        sibling = pick(target * iota(Z, 1).astype(F32), here)
        unit = pick(target, here * ahead)
        table_ref[0:Z, :] = (4.0 * sibling + unit).astype(I32)

    def find_sources():
        wanted = iota(HEAD, 0) + z * (X * S)
        row = iota(8, 0)
        total = jnp.zeros((8, HEAD), F32)
        for plane in range(Z):
            position, filled = decode(by_plane[plane : plane + 1, :])
            values = jnp.where(row == 0, float(plane), jnp.where(row == 1, offsets[plane : plane + 1, :], filled.astype(F32)))
            total = total + pick(values, (position == wanted).astype(F32))
        found[...] = total

    def find_deliveries():
        plane, offset, filled = found[0:1, :], found[1:2, :], found[2:3, :].astype(I32)
        slot, row = iota(1, 1) & (S - 1), iota(8, 0)
        comes = [units_on(lane, slot, filled).astype(F32) for lane in range(X)]
        leaves = units_on(x, slot, filled).astype(F32)
        stacked = jnp.broadcast_to(leaves, (8, HEAD))
        for lane in range(X):
            stacked = jnp.where(row == lane, comes[lane], stacked)
        near = (iota(HEAD, 1) < iota(HEAD, 0)) & ((iota(HEAD, 1) >> 5) == (iota(HEAD, 0) >> 5))
        sums = pick(stacked, near.astype(F32))
        ahead = iota(HEAD, 0).astype(F32) - sums[4:5]
        here = ((ahead >= 0.0) & (ahead < leaves)).astype(F32)
        target = ((iota(8, 1) >> 5) == row).astype(F32)
        spot = 64.0 * pick(target * plane, here) + pick(target * (offset - sums[4:5]), here)
        table_ref[16:24, :] = (spot + pick(target, here) * iota(8, 1).astype(F32)).astype(I32)
        for j in range(X):
            lane = (slot + j) & 3
            first, count = jnp.zeros((1, HEAD), F32), jnp.zeros((1, HEAD), F32)
            for i in range(X):
                first = first + jnp.where(lane == i, sums[i : i + 1] + 128.0 * i, 0.0)
                count = count + jnp.where(lane == i, comes[i], 0.0)
            for k in range(LANE_UNITS):
                value = jnp.where(count > float(k), first + float(k), 128.0 * X)
                table_ref[24 + 4 * k + j : 25 + 4 * k + j, :] = value.astype(I32)

    def find_largest():
        position, counts = pairs()
        largest = jnp.zeros((Z, 1), I32)
        for plane in range(Z):
            for count in counts:
                largest = larger(largest, jnp.sum(jnp.where((position >> 7) == plane, count, 0.0), axis=1, keepdims=True))
        largest = jnp.max(largest.astype(F32), axis=0, keepdims=True).astype(I32)
        table_ref[40:41, :] = jnp.broadcast_to(largest, (1, HEAD))

    def find_most():
        position, counts = pairs()

        def one(replica, most):
            here = (position >> 5) == replica
            for count in counts:
                total = jnp.sum(jnp.sum(jnp.where(here, count, 0.0), axis=0, keepdims=True), axis=1, keepdims=True)
                most = larger(most, total)
            return most

        most = lax.fori_loop(0, Z * X, one, jnp.zeros((1, 1), I32))
        largest = table_ref[40:41, :]
        choice = jnp.zeros((1, HEAD), I32)
        for units, delivered in CAPACITIES[:-1]:
            choice = choice + ((largest > units) | (most > delivered)).astype(I32)
        table_ref[41:48, :] = jnp.broadcast_to(choice, (7, HEAD))

    between = [gather_facts, find_offsets, find_sources, find_deliveries, find_largest, find_most]
    for wave in range(QUARTERS, QUARTERS + FORWARD - 1):
        turn_ring(wave)
        if between:
            between.pop(0)()
    for part in range(QUARTERS):
        for forward in (True, False):
            steps = FORWARD if forward else BACK
            ring(steps - 1, part, forward).wait_recv()
            for step in range(steps):
                ring(step, part, forward).wait_send()
    for i in range(1, X):
        for quarter in range(S // QUARTER):
            x_copy(i, quarter).wait()
    own_split.wait()


def attend_call(facts, own_facts, pool, query, fresh, prompt):
    dma = pltpu.SemaphoreType.DMA
    return pl.pallas_call(
        attend_kernel,
        out_shape=(
            jax.ShapeDtypeStruct((Z, X, 1, HEAD), I32),
            jax.ShapeDtypeStruct((X, S, LANE_UNITS, 16, HEAD), BF16),
            jax.ShapeDtypeStruct((Z, QUARTERS, 8, 2 * QUARTER, HEAD), BF16),
            jax.ShapeDtypeStruct((X, Z * S), I32),
            jax.ShapeDtypeStruct((48, HEAD), I32),
        ),
        in_specs=[SM, VM] + [HB] * 4,
        out_specs=(VM,) * 5,
        scratch_shapes=[
            pltpu.VMEM(pool.shape, BF16),
            pltpu.VMEM(query.shape, BF16),
            pltpu.VMEM(fresh.shape, BF16),
            pltpu.VMEM(prompt.shape, BF16),
            pltpu.VMEM((S, UNITS, 16, HEAD), BF16),
            pltpu.VMEM((X, S, LANE_UNITS, 16, HEAD), BF16),
            pltpu.VMEM((8, 2 * QUARTER, HEAD), F32),
            pltpu.VMEM((4 * S, HEAD), F32),
            pltpu.VMEM((Z, HEAD), I32),
            pltpu.VMEM((Z, HEAD), F32),
            pltpu.VMEM((8, HEAD), F32),
            dma((4,)), dma((X,)), dma((X,)), dma((Z,)), dma((Z,)), dma((X, 4)), dma((X, 4)),
            *[dma((QUARTERS * FORWARD,))] * 4, dma((1,)),
        ],
        compiler_params=pltpu.CompilerParams(
            collective_id=1, has_side_effects=True, vmem_limit_bytes=60 << 20
        ),
        name="attend_and_gather",
    )(facts, own_facts, pool, query, fresh, prompt)


def move_kernel(
    capacity, delivery,
    table_ref, position_ref, xbuf_ref, gathered_ref, weight_ref,
    moved_ref, block_ref,
    packed, arrived, wide, product, columns, chunk, chunks, outgoing, incoming,
    z_send, z_recv, w_send, w_recv, c_send, c_recv, t_send, t_recv, d_send, d_recv, own_sem,
):
    z, x, t = place()
    barrier = pltpu.get_barrier_semaphore()

    @pl.loop(1, Z)
    def _(i):
        pl.semaphore_signal(barrier, inc=1, **to_replica(lax.rem(z + i, Z), x))

    for i in range(1, X):
        pl.semaphore_signal(barrier, inc=1, **to_replica(z, lax.rem(x + i, X)))
    for i in range(1, T):
        pl.semaphore_signal(barrier, inc=1, **to_tensor(lax.rem(t + i, T)))
    pl.semaphore_wait(barrier, Z + X + T - 3)

    def z_copy(i):
        plane = lax.rem(z + i, Z)
        return pltpu.make_async_remote_copy(
            packed.at[plane], arrived.at[z], z_send.at[i], z_recv.at[i], **to_replica(plane, x)
        )

    @pl.loop(0, Z)
    def _(n):
        i = Z // 2 + (n // 2) - lax.rem(n, 2) * n
        plane = lax.rem(z + i, Z)
        for c in range(capacity):
            packed[plane, c] = xbuf_ref[table_ref[plane, c]]

        @pl.when(i > 0)
        def _():
            z_copy(i).start()

    own_plane = pltpu.make_async_copy(packed.at[z], arrived.at[z], own_sem.at[0])
    own_plane.start()
    incoming[X, 0] = jnp.zeros((16, HEAD), BF16)

    def w_copy(i):
        return pltpu.make_async_remote_copy(
            weight_ref, wide.at[x], w_send.at[i], w_recv.at[i], **to_replica(z, lax.rem(x + i, X))
        )

    for i in range(1, X):
        w_copy(i).start()
    own_weight = pltpu.make_async_copy(weight_ref, wide.at[x], own_sem.at[3])
    own_weight.start()
    own_weight.wait()
    for i in range(1, X):
        w_copy(i).wait()

    def multiply(planes):
        blocks = [block[...] for _, block in planes]
        rows = [jnp.concatenate([b[:, h].reshape(2 * S, HEAD) for b in blocks], axis=0) for h in range(8)]
        rows = jnp.concatenate(rows, axis=1)
        for pair in range(X // 2):
            weight = jnp.concatenate([wide[2 * pair], wide[2 * pair + 1]], axis=1)
            out = jnp.dot(rows, weight, preferred_element_type=F32)
            out = out.reshape(4, QUARTERS, 2, QUARTER, 2 * HEAD)
            for k in range(2):
                part = out[:, :, k].reshape(4, S, 2 * HEAD).astype(BF16)
                for n, (plane, _) in enumerate(planes):
                    target = pl.ds(plane * S, S)
                    for i in range(2):
                        product[2 * pair + i, k, target, :] = part[n, :, i * HEAD : (i + 1) * HEAD]

    for group in range(0, Z, 4):
        multiply([(plane, gathered_ref.at[plane]) for plane in range(group, group + 4)])

    def c_copy(i):
        lane = lax.rem(x + i, X)
        return pltpu.make_async_remote_copy(
            product.at[lane], columns.at[x], c_send.at[i], c_recv.at[i], **to_replica(z, lane)
        )

    for i in range(1, X):
        c_copy(i).start()
    own_columns = pltpu.make_async_copy(product.at[x], columns.at[x], own_sem.at[1])
    own_columns.start()
    own_columns.wait()
    for i in range(1, X):
        c_copy(i).wait()

    def t_copy(i):
        other = lax.rem(t + i, T)
        return pltpu.make_async_remote_copy(
            chunk.at[other], chunks.at[t], t_send.at[i], t_recv.at[i], **to_tensor(other)
        )

    @pl.loop(0, T)
    def _(n):
        i = lax.rem(n + 1, T)
        other = lax.rem(t + i, T)
        target = lax.broadcasted_iota(I32, (8 * S, Z * S), 0) + other * (8 * S)
        total = jnp.zeros((8 * S, 2 * HEAD), F32)
        for lane in range(X):
            pick = (position_ref[pl.ds(lane, 1), :] == target).astype(F32).astype(BF16)
            rows = jnp.concatenate([columns[lane, 0], columns[lane, 1]], axis=1)
            total = total + jnp.dot(pick, rows, preferred_element_type=F32)
        for k in range(2):
            chunk[other, k] = total[:, k * HEAD : (k + 1) * HEAD].astype(BF16)

        @pl.when(i > 0)
        def _():
            t_copy(i).start()

    own_chunk = pltpu.make_async_copy(chunk.at[t], chunks.at[t], own_sem.at[2])
    own_chunk.start()
    own_chunk.wait()
    for i in range(1, T):
        t_copy(i).wait()
    for k in range(2):
        total = chunks[0, k].astype(F32)
        for n in range(1, T):
            total = total + chunks[n, k].astype(F32)
        block_ref[k] = total.astype(BF16)

    own_plane.wait()

    @pl.loop(1, Z)
    def _(i):
        z_copy(i).wait()

    def d_copy(i):
        lane = lax.rem(x + i, X)
        return pltpu.make_async_remote_copy(
            outgoing.at[lane], incoming.at[x, pl.ds(0, delivery)], d_send.at[i], d_recv.at[i], **to_replica(z, lane)
        )

    @pl.loop(0, X)
    def _(n):
        i = lax.rem(n + 1, X)
        lane = lax.rem(x + i, X)

        @pl.loop(0, delivery // 8)
        def _(c):
            for j in range(8):
                index = table_ref[16 + lane, 8 * c + j]
                outgoing[lane, 8 * c + j] = arrived[index // 64, lax.rem(index, 64)]

        @pl.when(i > 0)
        def _():
            d_copy(i).start()

    own_delivery = pltpu.make_async_copy(outgoing.at[x], incoming.at[x, pl.ds(0, delivery)], own_sem.at[4])
    own_delivery.start()
    own_delivery.wait()
    for i in range(1, X):
        d_copy(i).wait()

    @pl.loop(0, S)
    def _(slot):
        for unit in range(UNITS):
            index = table_ref[24 + unit, x * S + slot]
            moved_ref[slot // 4, lax.rem(slot, 4), unit // 4, unit % 4] = incoming[index // 128, lax.rem(index, 128)]


def move_call(number, capacity, delivery, *operands):
    dma = pltpu.SemaphoreType.DMA
    return pl.pallas_call(
        functools.partial(move_kernel, capacity, delivery),
        out_shape=(
            jax.ShapeDtypeStruct((S // 4, 4, UNITS // 4, 4, 16, HEAD), BF16),
            jax.ShapeDtypeStruct((2, 8 * S, HEAD), BF16),
        ),
        in_specs=[SM, VM, VM, VM, HB],
        out_specs=(VM, VM),
        scratch_shapes=[
            pltpu.VMEM((Z, capacity, 16, HEAD), BF16),
            pltpu.VMEM((Z, capacity, 16, HEAD), BF16),
            pltpu.VMEM((X, 8 * HEAD, HEAD), BF16),
            pltpu.VMEM((X, 2, Z * S, HEAD), BF16),
            pltpu.VMEM((X, 2, Z * S, HEAD), BF16),
            pltpu.VMEM((T, 2, 8 * S, HEAD), BF16),
            pltpu.VMEM((T, 2, 8 * S, HEAD), BF16),
            pltpu.VMEM((X, delivery, 16, HEAD), BF16),
            pltpu.VMEM((X + 1, delivery, 16, HEAD), BF16),
            dma((Z,)), dma((Z,)), dma((X,)), dma((X,)), dma((X,)), dma((X,)), dma((T,)), dma((T,)),
            dma((X,)), dma((X,)), dma((5,)),
        ],
        compiler_params=pltpu.CompilerParams(
            collective_id=2 + number, has_side_effects=True, vmem_limit_bytes=48 << 20
        ),
        name="move_and_project",
    )(*operands)


def body(
    queries, fresh_entries, suffix_page_pool, page_table, suffix_len,
    prompt_key_value, prompt_len, sibling_group, new_position, output_weight,
):
    z, x, _ = place()
    numbers = jnp.concatenate(
        [page_table.T.reshape(-1) - (z * X + x) * (S * 8), new_position, suffix_len, sibling_group, prompt_len,
         jnp.zeros((30,), I32)]
    )
    own_facts = jnp.pad(new_position * 128 + suffix_len, (0, HEAD - S)).reshape(1, 1, HEAD)
    query = queries.reshape(S, 2, 8, HEAD).transpose(0, 2, 1, 3).reshape(S, 16, HEAD)
    _, xbuf, gathered, position, table = attend_call(
        numbers, own_facts, suffix_page_pool.reshape(S * 8, 32, HEAD), query,
        fresh_entries.reshape(4 * S, HEAD), prompt_key_value.reshape(2, 2 * 64, HEAD),
    )
    moved, block = lax.switch(
        table[41, 0], [functools.partial(move_call, n, c, d) for n, (c, d) in enumerate(CAPACITIES)],
        table, position, xbuf.reshape(X * S * LANE_UNITS, 16, HEAD), gathered, output_weight,
    )
    return moved.reshape(S, 128, 2, HEAD), block


def solution(mesh):
    placed = (
        P("replica", None, "tensor"),
        P("replica", None, None, "tensor"),
        P("replica", None, None, "tensor"),
        P("replica", None),
        P("replica"),
        P("replica", None, None, "tensor"),
        P("replica"),
        P("replica"),
        P("replica"),
        P("tensor", "replica"),
    )
    return jax.shard_map(
        body,
        mesh=mesh,
        in_specs=placed,
        out_specs=(P("replica", None, None, "tensor"), P(None, "tensor", "replica")),
        check_vma=False,
    )
```
